32 devices in a mesh: group: 4 (over x, core), seq: 4 (over z), tp: 2 (over y).
Axes of the slice: x: 2, y: 2, z: 4, core: 2. Of those that a mesh axis runs over, the one named last changes fastest.
Arguments:
- queries: bfloat16 [4, 512, 4096], P('seq', 'group', 'tp'), may hold values from -256 to 256
- keys: bfloat16 [4, 512, 512], P('seq', 'group', 'tp'), may hold values from -12 to 12
- values: bfloat16 [4, 512, 512], P('seq', 'group', 'tp'), may hold values from -6 to 6
- moe_x: bfloat16 [4, 128, 2048], P('group', ('seq', 'tp')), may hold values from -6 to 6
- expert_ids: int32 [4, 128, 8], P('group', ('seq', 'tp')), may hold values from 0 to 63, all different within a row; in each aligned block of 16 rows (0 to 15, 16 to 31, ..., all dimensions but the last counted through in order) at most 3 rows name the same one
- gates: float32 [4, 128, 8], P('group', ('seq', 'tp')), may hold values from 0.05 to 0.5
- grad_out: bfloat16 [4, 128, 2048], P('group', ('seq', 'tp')), may hold values from -6 to 6
- w_gate: bfloat16 [64, 2048, 384], P(('seq', 'tp')), may hold values from -0.125 to 0.125
- w_up: bfloat16 [64, 2048, 384], P(('seq', 'tp')), may hold values from -0.125 to 0.125
- w_down: bfloat16 [64, 384, 2048], P(('seq', 'tp')), may hold values from -0.3125 to 0.3125
Outputs:
- attn_out: bfloat16 [4, 512, 4096], P('seq', 'group', 'tp')
- moe_out: bfloat16 [4, 128, 2048], P('group', ('seq', 'tp'))
- moe_grad_in: bfloat16 [4, 128, 2048], P('group', ('seq', 'tp'))
The draws below stay inside these ranges and needn't reach their ends.
Inputs may be any that keep to these rules, and one draw needn't show every extreme that they name: `expert_ids`: each token names 8 different experts. Within each aligned block of 16 tokens (the tokens of one device, in order), no expert is named by more than 3 tokens, and in every draw some block names some expert exactly 3 times.
All inputs are finite; a program needn't handle non-finite values.
Results may differ from the reference program's by a relative error of at most 0.0064.
Values may be sent and summed in bfloat16 or wider, within the bound.
No kernel may reach another device: no remote copies, remote signals or barrier semaphores. Data moves between devices by JAX's collectives and lax.ppermute only.
A program may use at most 128 MiB of HBM per device.

```python
import math
import jax
import jax.numpy as jnp
import numpy as np
from jax import lax

D = 2048
H = 32
KVH = 4
HD = 128
TOPK = 8
EXPERTS = 64
FFE = 384
MOE_TOK = 16
CAP = 3
SEQ = 512
BATCH = 4
GROUP_TOK = 128
N_GROUP = 4
N_SEQ = 4
N_TP = 2


def drawn_pair(key):
    base_key = jax.random.fold_in(key, 7)
    key_part, query_part = jax.random.split(base_key, 2)
    key_rows = jax.random.truncated_normal(key_part, -4.0, 4.0, (BATCH, SEQ, KVH, HD), jnp.float32)
    query_rows = jax.random.truncated_normal(query_part, -4.0, 4.0, (BATCH, SEQ, H, HD), jnp.float32)
    return (key_rows, query_rows)


def draw_queries(key, part):
    key_rows, query_rows = drawn_pair(key)
    return query_rows.reshape(BATCH, SEQ, H * HD).astype(jnp.bfloat16)


def draw_keys(key, part):
    key_rows, query_rows = drawn_pair(key)
    return key_rows.reshape(BATCH, SEQ, KVH * HD).astype(jnp.bfloat16)


def levels(own_key, extent, cuts, low, largest):
    def one(axis_at, blocks):
        draws = jax.random.uniform(jax.random.fold_in(jax.random.fold_in(own_key, 6), axis_at), (blocks,), jnp.float32, low / len(cuts), largest / len(cuts))
        return jnp.repeat(jnp.exp(draws), extent[axis_at] // blocks).reshape((-1,) + (1,) * (len(extent) - axis_at - 1))

    factor_of = one(*cuts[0])
    for cut in cuts[1:]:
        factor_of = factor_of * one(*cut)
    return factor_of


def deal_out(key, own, number, rows, amount, top, bound, lean):
    ranking = jax.random.permutation(key, amount)
    heavy_load, common = shares(amount, rows * top, bound, lean, True), shares(amount, rows * top, bound, lean, False)
    places = jnp.arange(amount)

    def named(tallies, offset_by):
        used = int((tallies > 0).sum())
        fixed = max(1, used // 4)
        moved = fixed + (places - fixed + offset_by * (used - fixed)) % max(1, amount - fixed)
        return jnp.zeros((amount,), jnp.int32).at[ranking[jnp.where(places < fixed, places, moved)]].set(jnp.asarray(tallies, jnp.int32))

    tallies = jnp.where(number % 4 == 0, named(heavy_load, number // 4), named(common, number - number // 4 - 1))
    mixed = jax.random.permutation(jax.random.fold_in(own, 3), amount)
    donor, taker = mixed[0:amount // 2 * 2:2], mixed[1:amount // 2 * 2:2]
    slack = jnp.minimum(tallies[donor] - 1, bound - tallies[taker]) // 2
    slack = jnp.where((donor == ranking[0]) | (taker == ranking[0]) | (tallies[taker] == 0), 0, jnp.maximum(slack, 0))
    moved = jax.random.randint(jax.random.fold_in(own, 4), (amount // 2,), 0, 1 << 20) % (slack + 1)
    tallies = tallies.at[donor].add(-moved).at[taker].add(moved)
    members = jnp.searchsorted(jnp.cumsum(tallies), jnp.arange(rows * top), side="right").astype(jnp.int32)
    listing = members.reshape(top, rows).T
    listing = listing[jax.random.permutation(jax.random.fold_in(own, 1), rows)]
    offset_by = jax.random.randint(jax.random.fold_in(own, 2), (rows, 1), 0, top)
    return jnp.take_along_axis(listing, (jnp.arange(top)[None, :] + offset_by) % top, axis=1)


def shares(number_of, total, reach, lean, full):
    portions = [(1 << 20) // math.isqrt(grade ** lean) + 1 for grade in range(1, number_of + 1)]
    largest = reach if full else min(reach, max(-(-total // number_of), total * portions[0] // sum(portions)))
    least = 1 if total - largest >= number_of - 1 else 0
    given, surplus = [largest] + [least] * (number_of - 1), total - largest - least * (number_of - 1)
    while surplus > 0:
        free = [i for i in range(1, number_of) if given[i] < largest] or [i for i in range(1, number_of) if given[i] < reach]
        pool, budget = sum([portions[i] for i in free]), surplus
        for i in free:
            more = min(reach - given[i], max(1, budget * portions[i] // pool), surplus)
            given[i] = given[i] + more
            surplus = surplus - more
    return np.array(given)


def gaussian(own_key, shape, scale, most, cuts=(), held_as=jnp.bfloat16):
    loudness = levels(own_key, shape, cuts, -0.22, 0.18) if cuts else 1.0
    array = jax.random.normal(own_key, shape, jnp.float32) * scale * loudness
    return jnp.minimum(jnp.maximum(array, -most), most).astype(held_as)


def setup_inputs(seed: int = 0) -> dict:
    streams_of = jax.random.split(jax.random.key(seed), 11)
    queries = draw_queries(jax.random.fold_in(streams_of[10], 71), 0)
    keys = draw_keys(jax.random.fold_in(streams_of[10], 71), 0)
    values = gaussian(streams_of[2], (BATCH, SEQ, KVH * HD), 1.0, 6.0, ((0, 4), (1, 4), (2, 2)))
    moe_x = gaussian(streams_of[3], (N_GROUP, GROUP_TOK, D), 1.0, 6.0, ((0, 4), (1, 8)))
    expert_ids_keys = jax.random.split(jax.random.fold_in(streams_of[4], 1), N_GROUP * GROUP_TOK // MOE_TOK)
    expert_ids_turns = jax.random.permutation(jax.random.fold_in(streams_of[4], 3), N_GROUP * GROUP_TOK // MOE_TOK)
    expert_ids = jax.vmap(lambda own, number: deal_out(jax.random.fold_in(streams_of[4], 2), own, number, MOE_TOK, EXPERTS, TOPK, CAP, 2))(expert_ids_keys, expert_ids_turns).reshape((N_GROUP, GROUP_TOK, TOPK))
    gates = jnp.clip(jnp.exp(math.log(0.5) - 2.3025851 * jax.random.uniform(streams_of[5], (N_GROUP, GROUP_TOK, TOPK), jnp.float32) ** levels(streams_of[5], (N_GROUP, GROUP_TOK, TOPK), ((0, 4), (1, 8)), -0.2, 0.2)), 0.05, 0.5)
    grad_out = gaussian(streams_of[6], (N_GROUP, GROUP_TOK, D), 1.0, 6.0, ((0, 4), (1, 8)))
    w_gate = gaussian(streams_of[7], (EXPERTS, D, FFE), D ** -0.5, 0.125, ((0, 8),))
    w_up = gaussian(streams_of[8], (EXPERTS, D, FFE), D ** -0.5, 0.125, ((0, 8),))
    w_down = gaussian(streams_of[9], (EXPERTS, FFE, D), FFE ** -0.5, 0.3125, ((0, 8),))
    return {"queries": queries, "keys": keys, "values": values, "moe_x": moe_x, "expert_ids": expert_ids, "gates": gates, "grad_out": grad_out, "w_gate": w_gate, "w_up": w_up, "w_down": w_down}


def attend_head(query_rows, key_rows, value_rows):
    seq_len = query_rows.shape[0]
    block_len = min(512, seq_len)
    score_scale = 1.0 / (query_rows.shape[1] ** 0.5)
    pieces = []
    for first_row in range(0, seq_len, block_len):
        last_row = first_row + block_len
        scores = lax.dot_general(query_rows[first_row:last_row], key_rows[:last_row], (((1,), (1,)), ((), ())), preferred_element_type=jnp.float32) * score_scale
        row_pos = first_row + lax.broadcasted_iota(jnp.int32, (block_len, last_row), 0)
        col_pos = lax.broadcasted_iota(jnp.int32, (block_len, last_row), 1)
        scores = jnp.where(col_pos <= row_pos, scores, -jnp.inf)
        row_max = jnp.max(scores, axis=1, keepdims=True)
        exp_scores = jnp.exp(scores - row_max)
        row_total = jnp.sum(exp_scores, axis=1, keepdims=True)
        mixed_rows = jnp.dot(exp_scores.astype(jnp.bfloat16), value_rows[:last_row], preferred_element_type=jnp.float32)
        pieces.append((mixed_rows / row_total).astype(jnp.bfloat16))
    return jnp.concatenate(pieces, axis=0)


def attention(queries, keys, values):
    group_len = H // KVH

    def one_head(flat_index):
        batch_idx = flat_index // H
        head_idx = flat_index % H
        kv_head = head_idx // group_len
        query_seq = lax.dynamic_index_in_dim(queries, batch_idx, 0, False)
        key_seq = lax.dynamic_index_in_dim(keys, batch_idx, 0, False)
        value_seq = lax.dynamic_index_in_dim(values, batch_idx, 0, False)
        query_rows = lax.dynamic_slice_in_dim(query_seq, (head_idx * HD).astype(jnp.int32), HD, 1)
        key_rows = lax.dynamic_slice_in_dim(key_seq, (kv_head * HD).astype(jnp.int32), HD, 1)
        value_rows = lax.dynamic_slice_in_dim(value_seq, (kv_head * HD).astype(jnp.int32), HD, 1)
        return attend_head(query_rows, key_rows, value_rows)

    stacked = lax.map(one_head, jnp.arange(BATCH * H, dtype=jnp.int32))
    return stacked.reshape(BATCH, H, SEQ, HD).transpose(0, 2, 1, 3).reshape(BATCH, SEQ, H * HD)


def expert_rows(token_rows, grad_rows, gate_proj, up_proj, down_proj):
    hgate = jnp.dot(token_rows, gate_proj, preferred_element_type=jnp.float32)
    hup = jnp.dot(token_rows, up_proj, preferred_element_type=jnp.float32)
    sigmoid_gate = jax.nn.sigmoid(hgate)
    silu_gate = hgate * sigmoid_gate
    activated = (silu_gate * hup).astype(jnp.bfloat16)
    expert_out = jnp.dot(activated, down_proj, preferred_element_type=jnp.float32).astype(jnp.bfloat16)
    grad_act = lax.dot_general(grad_rows, down_proj, (((1,), (1,)), ((), ())), preferred_element_type=jnp.float32)
    grad_gate = (grad_act * hup * sigmoid_gate * (1.0 + hgate * (1.0 - sigmoid_gate))).astype(jnp.bfloat16)
    grad_up = (grad_act * silu_gate).astype(jnp.bfloat16)
    input_grad = lax.dot_general(grad_gate, gate_proj, (((1,), (1,)), ((), ())), preferred_element_type=jnp.float32)
    input_grad = input_grad + lax.dot_general(grad_up, up_proj, (((1,), (1,)), ((), ())), preferred_element_type=jnp.float32)
    return expert_out, input_grad.astype(jnp.bfloat16)


def experts_layer(moe_x, expert_ids, gates, grad_out, w_gate, w_up, w_down):
    devices = N_SEQ * N_TP
    slots = devices * CAP

    def one_batch(batch_idx):
        token_x = lax.dynamic_index_in_dim(moe_x, batch_idx, 0, False)
        route_ids = lax.dynamic_index_in_dim(expert_ids, batch_idx, 0, False)
        route_gates = lax.dynamic_index_in_dim(gates, batch_idx, 0, False)
        token_grad = lax.dynamic_index_in_dim(grad_out, batch_idx, 0, False)
        owner_ids = route_ids.reshape(devices, MOE_TOK * TOPK)
        onehot = (owner_ids[:, :, None] == jnp.arange(EXPERTS, dtype=jnp.int32)[None, None, :]).astype(jnp.int32)
        before = jnp.cumsum(onehot, axis=1) - onehot
        rank_in = jnp.sum(before * onehot, axis=2)
        device_ids = jnp.arange(devices, dtype=jnp.int32)[:, None]
        slot_place = (owner_ids * slots + device_ids * CAP + rank_in).reshape(-1).astype(jnp.int32)
        token_ids = (jnp.arange(devices * MOE_TOK * TOPK, dtype=jnp.int32) // TOPK).astype(jnp.int32)
        token_table = jnp.zeros((EXPERTS * slots,), jnp.int32).at[slot_place].set(token_ids)
        gate_table = jnp.zeros((EXPERTS * slots,), jnp.float32).at[slot_place].set(route_gates.reshape(-1))
        live_table = jnp.zeros((EXPERTS * slots,), jnp.float32).at[slot_place].set(1.0)
        token_table = token_table.reshape(EXPERTS, slots)
        gate_table = gate_table.reshape(EXPERTS, slots)
        live_table = live_table.reshape(EXPERTS, slots)

        def one_expert(expert_idx):
            slot_tokens = token_table[expert_idx]
            token_rows = jnp.where(live_table[expert_idx][:, None] > 0, token_x[slot_tokens], jnp.zeros((), jnp.bfloat16))
            grad_rows = (gate_table[expert_idx][:, None] * token_grad[slot_tokens].astype(jnp.float32)).astype(jnp.bfloat16)
            return expert_rows(token_rows, grad_rows, w_gate[expert_idx], w_up[expert_idx], w_down[expert_idx])

        outs_all, grads_all = lax.map(one_expert, jnp.arange(EXPERTS, dtype=jnp.int32))
        flat_tokens = token_table.reshape(-1)
        mixed = jnp.zeros((GROUP_TOK, D), jnp.float32).at[flat_tokens].add(gate_table.reshape(-1)[:, None] * outs_all.reshape(-1, D).astype(jnp.float32))
        summed = jnp.zeros((GROUP_TOK, D), jnp.float32).at[flat_tokens].add(live_table.reshape(-1)[:, None] * grads_all.reshape(-1, D).astype(jnp.float32))
        return mixed.astype(jnp.bfloat16), summed.astype(jnp.bfloat16)

    return lax.map(one_batch, jnp.arange(N_GROUP, dtype=jnp.int32))


def reference(queries, keys, values, moe_x, expert_ids, gates, grad_out, w_gate, w_up, w_down):
    attn_out = attention(queries, keys, values)
    moe_out, moe_grad_in = experts_layer(moe_x, expert_ids, gates, grad_out, w_gate, w_up, w_down)
    return (attn_out, moe_out, moe_grad_in)
```

```python
import functools

import jax
import jax.numpy as jnp
from jax import lax
from jax.experimental import pallas as pl
from jax.experimental.pallas import tpu as pltpu
from jax.sharding import PartitionSpec as P

H = 32
KVH = 4
HD = 128
EXPERTS = 64
NT = (((1,), (1,)), ((), ()))
VMEM = pl.BlockSpec(memory_space=pltpu.VMEM)
SMEM = pl.BlockSpec(memory_space=pltpu.SMEM)
F32 = jnp.float32
BF16 = jnp.bfloat16


def swap(array, axis, offset):
    count = lax.axis_size(axis)
    return lax.ppermute(array, axis, [(i, i ^ offset) for i in range(count)])


def pack_kernel(ids_ref, gates_ref, x_ref, out_ref):
    rows, width = x_ref.shape
    topk = ids_ref.shape[0]
    expert = lax.broadcasted_iota(jnp.int32, (EXPERTS, rows), 0)
    table = jnp.zeros((EXPERTS, rows), F32)
    for k in range(topk):
        table = table + jnp.where(ids_ref[k : k + 1] == expert, gates_ref[k : k + 1], 0.0)
    high = table.astype(BF16).astype(F32)
    low = table - high
    both = jnp.concatenate([high, low], axis=0)
    out_ref[:, :width] = x_ref[...]
    out_ref[:, width:] = jnp.transpose(both).astype(BF16)


def pack_rows(ids, gates, x):
    rows, width = x.shape
    return pl.pallas_call(
        pack_kernel,
        in_specs=[VMEM] * 3,
        out_specs=VMEM,
        out_shape=jax.ShapeDtypeStruct((rows, width + 2 * EXPERTS), BF16),
        name="pack_rows",
    )(ids, gates, x)


def attention_kernel(base_ref, q_ref, *refs):
    out_ref = refs[-1]
    kv_refs = refs[:-1]
    rows, width = q_ref.shape
    half = kv_refs[0].shape[1] // 2
    kv_heads = half // HD
    heads = width // HD
    repeat = heads // kv_heads
    scale = 1.0 / HD**0.5
    pieces = len(kv_refs)
    row_pos = base_ref[0] * rows + lax.broadcasted_iota(jnp.int32, (rows, rows), 0)
    col_pos = lax.broadcasted_iota(jnp.int32, (rows, rows), 1)
    bias = jnp.concatenate(
        [
            jnp.where(col_pos + base_ref[p] * rows <= row_pos, 0.0, -jnp.inf)
            for p in range(pieces)
        ],
        axis=1,
    )
    for g in range(kv_heads):
        keys = jnp.concatenate([r[:, g * HD : (g + 1) * HD] for r in kv_refs], axis=0)
        vals = jnp.concatenate(
            [r[:, half + g * HD : half + (g + 1) * HD] for r in kv_refs], axis=0
        )
        for h in range(g * repeat, (g + 1) * repeat):
            cols = slice(h * HD, (h + 1) * HD)
            scores = lax.dot_general(q_ref[:, cols], keys, NT, preferred_element_type=F32)
            scores = scores * scale + bias
            top = jnp.max(scores, axis=1, keepdims=True)
            exps = jnp.exp(scores - top)
            total = jnp.sum(exps, axis=1, keepdims=True)
            mixed = jnp.dot(exps.astype(BF16), vals, preferred_element_type=F32)
            out_ref[:, cols] = (mixed / total).astype(BF16)


def attend(base, q, kv):
    rows, width = q.shape
    keys = rows * len(kv)
    return pl.pallas_call(
        attention_kernel,
        in_specs=[SMEM] + [VMEM] * (1 + len(kv)),
        out_specs=VMEM,
        out_shape=jax.ShapeDtypeStruct((rows, width), BF16),
        cost_estimate=pl.CostEstimate(
            flops=4 * rows * keys * width, bytes_accessed=4 * rows * width, transcendentals=0
        ),
        name="attention",
    )(base, q, *kv)


def forward_kernel(shard_ref, *refs, count):
    x_refs = refs[:count]
    gate_ref, up_ref, down_ref = refs[count : count + 3]
    outs = refs[count + 3 : 2 * count + 3]
    silu_ref, rest_ref = refs[2 * count + 3 : 2 * count + 5]
    rows_scr, gates_scr, act_scr = refs[-3:]
    local, width, _ = gate_ref.shape
    piece = x_refs[0].shape[0]
    tokens = count * piece
    for p in range(count):
        rows_scr[p * piece : (p + 1) * piece] = x_refs[p][:, :width]
        gates_scr[p * piece : (p + 1) * piece] = x_refs[p][:, width:]
    lane = lax.broadcasted_iota(jnp.int32, gates_scr.shape, 1)

    @pl.loop(0, local)
    def _(e):
        col = shard_ref[0] * local + e
        gates = gates_scr[...].astype(F32)
        mine = jnp.sum(
            jnp.where((lane == col) | (lane == col + EXPERTS), gates, 0.0), axis=1, keepdims=True
        )
        hgate = jnp.dot(rows_scr[...], gate_ref[e], preferred_element_type=F32)
        hup = jnp.dot(rows_scr[...], up_ref[e], preferred_element_type=F32)
        sig = jax.nn.sigmoid(hgate)
        silu = hgate * sig * mine
        silu_ref[e] = silu
        rest_ref[e] = hup * sig * (1.0 + hgate * (1.0 - sig)) * mine
        act_scr[e] = (silu * hup).astype(BF16)

    chunk = 256

    @pl.loop(0, width // chunk)
    def _(c):
        cols = pl.ds(pl.multiple_of(c * chunk, chunk), chunk)
        total = jnp.zeros((tokens, chunk), F32)
        for e in range(local):
            total = total + jnp.dot(act_scr[e], down_ref[e, :, cols], preferred_element_type=F32)
        total = total.astype(BF16)
        for p in range(count):
            outs[p][:, cols] = total[p * piece : (p + 1) * piece]


def experts_forward(shard, pieces, w_gate, w_up, w_down):
    count = len(pieces)
    local, width, hidden = w_gate.shape
    piece = pieces[0].shape[0]
    tokens = count * piece
    shapes = [jax.ShapeDtypeStruct((piece, width), BF16)] * count
    shapes += [jax.ShapeDtypeStruct((local, tokens, hidden), F32)] * 2
    shapes += [jax.ShapeDtypeStruct(w.shape, w.dtype) for w in (w_gate, w_up, w_down)]

    def body(shard_ref, *refs):
        ins, outs = refs[: count + 3], refs[count + 3 : 2 * count + 5]
        forward_kernel(shard_ref, *ins, *outs, *refs[-3:], count=count)

    res = pl.pallas_call(
        body,
        in_specs=[SMEM] + [VMEM] * (count + 3),
        out_specs=[VMEM] * (count + 5),
        out_shape=shapes,
        input_output_aliases={1 + count + i: count + 2 + i for i in range(3)},
        scratch_shapes=[
            pltpu.VMEM((tokens, width), BF16),
            pltpu.VMEM((tokens, pieces[0].shape[1] - width), BF16),
            pltpu.VMEM((local, tokens, hidden), BF16),
        ],
        compiler_params=pltpu.CompilerParams(vmem_limit_bytes=16 * 2**20),
        cost_estimate=pl.CostEstimate(
            flops=6 * tokens * local * width * hidden,
            bytes_accessed=6 * local * width * hidden,
            transcendentals=0,
        ),
        name="experts_forward",
    )(shard, *pieces, w_gate, w_up, w_down)
    return res[:count], res[count], res[count + 1], res[count + 2 :]


def backward_kernel(*refs, count):
    g_refs = refs[:count]
    gate_ref, up_ref, down_ref, silu_ref, rest_ref = refs[count : count + 5]
    outs = refs[count + 5 : 2 * count + 5]
    rows_scr, gate_scr, up_scr = refs[-3:]
    local, width, _ = gate_ref.shape
    piece = g_refs[0].shape[0]
    tokens = count * piece
    for p in range(count):
        rows_scr[p * piece : (p + 1) * piece] = g_refs[p][...]

    @pl.loop(0, local)
    def _(e):
        grad_act = lax.dot_general(rows_scr[...], down_ref[e], NT, preferred_element_type=F32)
        gate_scr[e] = (grad_act * rest_ref[e]).astype(BF16)
        up_scr[e] = (grad_act * silu_ref[e]).astype(BF16)

    chunk = 256

    @pl.loop(0, width // chunk)
    def _(c):
        cols = pl.ds(pl.multiple_of(c * chunk, chunk), chunk)
        total = jnp.zeros((tokens, chunk), F32)
        for e in range(local):
            total = total + lax.dot_general(
                gate_scr[e], gate_ref[e, cols, :], NT, preferred_element_type=F32
            )
            total = total + lax.dot_general(
                up_scr[e], up_ref[e, cols, :], NT, preferred_element_type=F32
            )
        total = total.astype(BF16)
        for p in range(count):
            outs[p][:, cols] = total[p * piece : (p + 1) * piece]


def experts_backward(pieces, weights, silu, rest):
    count = len(pieces)
    local, width, hidden = weights[0].shape
    piece = pieces[0].shape[0]
    tokens = count * piece
    return pl.pallas_call(
        functools.partial(backward_kernel, count=count),
        in_specs=[VMEM] * (count + 5),
        out_specs=[VMEM] * count,
        out_shape=[jax.ShapeDtypeStruct((piece, width), BF16)] * count,
        scratch_shapes=[
            pltpu.VMEM((tokens, width), BF16),
            pltpu.VMEM((local, tokens, hidden), BF16),
            pltpu.VMEM((local, tokens, hidden), BF16),
        ],
        compiler_params=pltpu.CompilerParams(vmem_limit_bytes=16 * 2**20),
        cost_estimate=pl.CostEstimate(
            flops=6 * tokens * local * width * hidden,
            bytes_accessed=6 * local * width * hidden,
            transcendentals=0,
        ),
        name="experts_backward",
    )(*pieces, *weights, silu, rest)


def spread(rows):
    near = [rows] + [swap(rows, "seq", d) for d in range(1, lax.axis_size("seq"))]
    pieces = list(near)
    for t in range(1, lax.axis_size("tp")):
        pieces += [swap(a, "tp", t) for a in near]
    return pieces


def collect(pieces):
    seq, tp = lax.axis_size("seq"), lax.axis_size("tp")
    sums = []
    for d in range(seq):
        terms = [pieces[d]] + [swap(pieces[t * seq + d], "tp", t) for t in range(1, tp)]
        total = sum(a.astype(F32) for a in terms)
        sums.append(total if d == 0 else swap(total.astype(BF16), "seq", d).astype(F32))
    return sum(sums).astype(BF16)


def shards(queries, keys, values, moe_x, expert_ids, gates, grad_out, w_gate, w_up, w_down):
    group = lax.axis_index("group")
    weights = [pltpu.with_memory_space_constraint(w, pltpu.VMEM) for w in (w_gate, w_up, w_down)]
    shard = (lax.axis_index("seq") * lax.axis_size("tp") + lax.axis_index("tp")).reshape(1)
    x_pieces = spread(pack_rows(expert_ids[0].T, gates[0].T, moe_x[0]))
    g_pieces = spread(grad_out[0])
    kv = jnp.concatenate([keys[0], values[0]], axis=1)
    offsets = range(lax.axis_size("group"))
    kv_pieces = [kv] + [swap(kv, "group", d) for d in offsets[1:]]
    base = jnp.stack([group ^ d for d in offsets])
    attn_out = attend(base, queries[0], kv_pieces)
    outs, silu, rest, weights = experts_forward(shard, x_pieces, *weights)
    moe_out = collect(outs)
    moe_grad_in = collect(experts_backward(g_pieces, weights, silu, rest))
    return attn_out[None], moe_out[None], moe_grad_in[None]


def solution(mesh):
    rows = P("seq", "group", "tp")
    tokens = P("group", ("seq", "tp"), None)
    experts = P(("seq", "tp"), None, None)
    return jax.shard_map(
        shards,
        mesh=mesh,
        in_specs=(rows, rows, rows, tokens, tokens, tokens, tokens, experts, experts, experts),
        out_specs=(rows, tokens, tokens),
        check_vma=False,
    )
```

```python
import functools

import jax
import jax.numpy as jnp
from jax import lax
from jax.experimental import pallas as pl
from jax.experimental.pallas import tpu as pltpu
from jax.sharding import PartitionSpec as P

H = 32
KVH = 4
HD = 128
EXPERTS = 64
CAP = 3
NT = (((1,), (1,)), ((), ()))
VMEM = pl.BlockSpec(memory_space=pltpu.VMEM)
SMEM = pl.BlockSpec(memory_space=pltpu.SMEM)
F32 = jnp.float32
BF16 = jnp.bfloat16


def swap(array, axis, offset):
    count = lax.axis_size(axis)
    return lax.ppermute(array, axis, [(i, i ^ offset) for i in range(count)])


def pack_kernel(ids_ref, gates_ref, x_ref, grad_ref, out_ref):
    rows, width = x_ref.shape
    topk = ids_ref.shape[0]
    expert = lax.broadcasted_iota(jnp.int32, (EXPERTS, rows), 0)
    table = jnp.zeros((EXPERTS, rows), F32)
    for k in range(topk):
        table = table + jnp.where(ids_ref[k : k + 1] == expert, gates_ref[k : k + 1], 0.0)
    high = table.astype(BF16).astype(F32)
    both = jnp.concatenate([high, table - high], axis=0)
    out_ref[:, :width] = x_ref[...]
    out_ref[:, width : 2 * width] = grad_ref[...]
    out_ref[:, 2 * width :] = jnp.transpose(both).astype(BF16)


def pack_rows(ids, gates, x, grad):
    rows, width = x.shape
    return pl.pallas_call(
        pack_kernel,
        in_specs=[VMEM] * 4,
        out_specs=VMEM,
        out_shape=jax.ShapeDtypeStruct((rows, 2 * (width + EXPERTS)), BF16),
        name="pack_rows",
    )(ids, gates, x, grad)


def attention_kernel(base_ref, q_ref, *refs):
    out_ref = refs[-1]
    kv_refs = refs[:-1]
    rows, width = q_ref.shape
    half = kv_refs[0].shape[1] // 2
    kv_heads = half // HD
    heads = width // HD
    repeat = heads // kv_heads
    scale = 1.0 / HD**0.5
    pieces = len(kv_refs)
    row_pos = base_ref[0] * rows + lax.broadcasted_iota(jnp.int32, (rows, rows), 0)
    col_pos = lax.broadcasted_iota(jnp.int32, (rows, rows), 1)
    bias = jnp.concatenate(
        [
            jnp.where(col_pos + base_ref[p] * rows <= row_pos, 0.0, -jnp.inf)
            for p in range(pieces)
        ],
        axis=1,
    )
    for g in range(kv_heads):
        keys = jnp.concatenate([r[:, g * HD : (g + 1) * HD] for r in kv_refs], axis=0)
        vals = jnp.concatenate(
            [r[:, half + g * HD : half + (g + 1) * HD] for r in kv_refs], axis=0
        )
        for h in range(g * repeat, (g + 1) * repeat):
            cols = slice(h * HD, (h + 1) * HD)
            scores = lax.dot_general(q_ref[:, cols], keys, NT, preferred_element_type=F32)
            scores = scores * scale + bias
            top = jnp.max(scores, axis=1, keepdims=True)
            exps = jnp.exp(scores - top)
            total = jnp.sum(exps, axis=1, keepdims=True)
            mixed = jnp.dot(exps.astype(BF16), vals, preferred_element_type=F32)
            out_ref[:, cols] = (mixed / total).astype(BF16)


def attend(base, q, kv):
    rows, width = q.shape
    keys = rows * len(kv)
    return pl.pallas_call(
        attention_kernel,
        in_specs=[SMEM] + [VMEM] * (1 + len(kv)),
        out_specs=VMEM,
        out_shape=jax.ShapeDtypeStruct((rows, width), BF16),
        cost_estimate=pl.CostEstimate(
            flops=4 * rows * keys * width, bytes_accessed=4 * rows * width, transcendentals=0
        ),
        name="attention",
    )(base, q, *kv)


def routing_rows(shard, gates, local, slots):
    tokens, lanes = gates.shape
    lane = lax.broadcasted_iota(jnp.int32, (local, lanes), 1)
    mine = shard * local + lax.broadcasted_iota(jnp.int32, (local, lanes), 0)
    columns = ((lane == mine) | (lane == mine + EXPERTS)).astype(BF16)
    weight = lax.dot_general(columns, gates, NT, preferred_element_type=F32)
    live = weight > 0
    earlier = lax.broadcasted_iota(jnp.int32, (tokens, tokens), 0)
    earlier = (earlier < lax.broadcasted_iota(jnp.int32, (tokens, tokens), 1)).astype(BF16)
    rank = jnp.dot(live.astype(BF16), earlier, preferred_element_type=F32)
    slot = lax.broadcasted_iota(jnp.int32, (slots, tokens), 0).astype(F32)
    picks, scales = [], []
    for e in range(local):
        pick = jnp.where((slot == rank[e : e + 1]) & live[e : e + 1], 1.0, 0.0)
        picks.append(pick)
        scales.append(jnp.sum(pick * weight[e : e + 1], axis=1, keepdims=True))
    return jnp.concatenate(picks, axis=0), jnp.concatenate(scales, axis=0)


def experts_kernel(shard_ref, *refs, count, slots):
    pieces = refs[:count]
    weights = refs[count : count + 3]
    outs = refs[count + 3 : 2 * count + 3]
    held, sems, tokens_scr, rows_scr, back_scr, scale_scr, pick_scr = refs[2 * count + 3 :]
    gate_scr, up_scr, down_scr = held
    local, width, hidden = gate_scr.shape
    piece = pieces[0].shape[0]
    both = 2 * width

    def copy(which, e):
        return pltpu.make_async_copy(
            weights[which].at[e], held[which].at[e], sems.at[which, e]
        )

    for e in range(local):
        for which in range(3):
            copy(which, e).start()

    for p in range(count):
        tokens_scr[p * piece : (p + 1) * piece] = pieces[p][:, :both]
    gates = jnp.concatenate([r[:, both:] for r in pieces], axis=0)
    picks, scales = routing_rows(shard_ref[0], gates, local, slots)
    scale_scr[...] = jnp.broadcast_to(scales, scale_scr.shape)
    high = scales.astype(BF16).astype(F32)
    for i, part in enumerate((picks, picks * high, picks * (scales - high))):
        pick_scr[i] = jnp.transpose(part).astype(BF16)
    picks = picks.astype(BF16)
    chunk = 512
    for c in range(0, both, chunk):
        rows_scr[:, c : c + chunk] = jnp.dot(
            picks, tokens_scr[:, c : c + chunk], preferred_element_type=F32
        ).astype(BF16)

    @pl.loop(0, local)
    def _(e):
        mine = pl.ds(pl.multiple_of(e * slots, slots), slots)
        for which in range(3):
            copy(which, e).wait()
        scale = scale_scr[mine, :1]
        entry = jnp.concatenate([gate_scr[e], up_scr[e]], axis=1)
        hidden_both = jnp.dot(rows_scr[mine, :width], entry, preferred_element_type=F32)
        hgate, hup = hidden_both[:, :hidden], hidden_both[:, hidden:]
        sig = jax.nn.sigmoid(hgate)
        silu = hgate * sig
        activated = (silu * hup).astype(BF16)
        back_scr[mine, :width] = jnp.dot(
            activated, down_scr[e], preferred_element_type=F32
        ).astype(BF16)
        row_grad = (rows_scr[mine, width:].astype(F32) * scale).astype(BF16)
        grad_act = lax.dot_general(row_grad, down_scr[e], NT, preferred_element_type=F32)
        grad_gate = (grad_act * hup * sig * (1.0 + hgate * (1.0 - sig))).astype(BF16)
        grad_up = (grad_act * silu).astype(BF16)
        grads = jnp.concatenate([grad_gate, grad_up], axis=1)
        entry = jnp.concatenate([gate_scr[e], up_scr[e]], axis=1)
        back_scr[mine, width:] = lax.dot_general(
            grads, entry, NT, preferred_element_type=F32
        ).astype(BF16)

    for c in range(0, both, chunk):
        rows = back_scr[:, c : c + chunk]
        if c < width:
            total = jnp.dot(pick_scr[1], rows, preferred_element_type=F32)
            total = total + jnp.dot(pick_scr[2], rows, preferred_element_type=F32)
        else:
            total = jnp.dot(pick_scr[0], rows, preferred_element_type=F32)
        total = total.astype(BF16)
        for p in range(count):
            outs[p][:, c : c + chunk] = total[p * piece : (p + 1) * piece]


def experts(shard, pieces, w_gate, w_up, w_down):
    count = len(pieces)
    local, width, hidden = w_gate.shape
    piece = pieces[0].shape[0]
    tokens = count * piece
    slots = -(-CAP * count // 16) * 16
    scratch = [
        tuple(pltpu.VMEM(w.shape, BF16) for w in (w_gate, w_up, w_down)),
        pltpu.SemaphoreType.DMA((3, local)),
        pltpu.VMEM((tokens, 2 * width), BF16),
        pltpu.VMEM((local * slots, 2 * width), BF16),
        pltpu.VMEM((local * slots, 2 * width), BF16),
        pltpu.VMEM((local * slots, 128), F32),
        pltpu.VMEM((3, tokens, local * slots), BF16),
    ]
    held_bytes = 6 * local * width * hidden + 4 * width * (tokens + 2 * local * slots)
    return pl.pallas_call(
        functools.partial(experts_kernel, count=count, slots=slots),
        in_specs=[SMEM] + [VMEM] * count + [pl.BlockSpec(memory_space=pl.ANY)] * 3,
        out_specs=[VMEM] * count,
        out_shape=[jax.ShapeDtypeStruct((piece, 2 * width), BF16)] * count,
        scratch_shapes=scratch,
        compiler_params=pltpu.CompilerParams(vmem_limit_bytes=held_bytes + 10 * 2**20),
        cost_estimate=pl.CostEstimate(
            flops=12 * local * slots * width * hidden,
            bytes_accessed=6 * local * width * hidden,
            transcendentals=0,
        ),
        name="experts",
    )(shard, *pieces, w_gate, w_up, w_down)


def parent(offset):
    return offset & (offset - 1)


def spread(rows):
    near = [rows]
    for d in range(1, lax.axis_size("seq")):
        near.append(swap(near[parent(d)], "seq", d - parent(d)))
    pieces = list(near)
    for t in range(1, lax.axis_size("tp")):
        pieces += [swap(a, "tp", t) for a in near]
    return pieces


def collect(pieces):
    seq, tp = lax.axis_size("seq"), lax.axis_size("tp")
    terms = [[pieces[d]] for d in range(seq)]
    for d in reversed(range(seq)):
        terms[d] += [swap(pieces[t * seq + d], "tp", t) for t in range(1, tp)]
        total = sum(a.astype(F32) for a in terms[d]).astype(BF16)
        if d:
            terms[d] = []
            terms[parent(d)].append(swap(total, "seq", d - parent(d)))
        if d and d % 8 == 0:
            pieces, terms = lax.optimization_barrier((pieces, terms))
    return total


def shards(queries, keys, values, moe_x, expert_ids, gates, grad_out, w_gate, w_up, w_down):
    group = lax.axis_index("group")
    shard = (lax.axis_index("seq") * lax.axis_size("tp") + lax.axis_index("tp")).reshape(1)
    pieces = spread(pack_rows(expert_ids[0].T, gates[0].T, moe_x[0], grad_out[0]))
    kv = jnp.concatenate([keys[0], values[0]], axis=1)
    offsets = range(lax.axis_size("group"))
    kv_pieces = [kv] + [swap(kv, "group", d) for d in offsets[1:]]
    base = jnp.stack([group ^ d for d in offsets])
    attn_out = attend(base, queries[0], kv_pieces)
    total = collect(experts(shard, pieces, w_gate, w_up, w_down))
    width = moe_x.shape[-1]
    return attn_out[None], total[None, :, :width], total[None, :, width:]


def solution(mesh):
    rows = P("seq", "group", "tp")
    tokens = P("group", ("seq", "tp"), None)
    experts = P(("seq", "tp"), None, None)
    return jax.shard_map(
        shards,
        mesh=mesh,
        in_specs=(rows, rows, rows, tokens, tokens, tokens, tokens, experts, experts, experts),
        out_specs=(rows, tokens, tokens),
        check_vma=False,
    )
```

```python
import functools
import math

import jax
import jax.numpy as jnp
from jax import lax
from jax.experimental import pallas as pl
from jax.experimental.pallas import tpu as pltpu
from jax.sharding import PartitionSpec as P

H = 32
KVH = 4
HD = 128
EXPERTS = 64
CAP = 3
NT = (((1,), (1,)), ((), ()))
VMEM = pl.BlockSpec(memory_space=pltpu.VMEM)
SMEM = pl.BlockSpec(memory_space=pltpu.SMEM)
F32 = jnp.float32
BF16 = jnp.bfloat16


def swap(array, axis, offset):
    count = lax.axis_size(axis)
    return lax.ppermute(array, axis, [(i, i ^ offset) for i in range(count)])


def pack_kernel(ids_ref, gates_ref, x_ref, grad_ref, key_ref, value_ref, out_ref, kv_ref):
    rows, width = x_ref.shape
    topk = ids_ref.shape[0]
    expert = lax.broadcasted_iota(jnp.int32, (EXPERTS, rows), 0)
    table = jnp.zeros((EXPERTS, rows), F32)
    for k in range(topk):
        table = table + jnp.where(ids_ref[k : k + 1] == expert, gates_ref[k : k + 1], 0.0)
    high = table.astype(BF16).astype(F32)
    both = jnp.concatenate([high, table - high], axis=0)
    out_ref[:, :width] = x_ref[...]
    out_ref[:, width : 2 * width] = grad_ref[...]
    out_ref[:, 2 * width :] = jnp.transpose(both).astype(BF16)
    half = key_ref.shape[1]
    kv_ref[:, :half] = key_ref[...]
    kv_ref[:, half:] = value_ref[...]


def pack(ids, gates, x, grad, keys, values):
    rows, width = x.shape
    return pl.pallas_call(
        pack_kernel,
        in_specs=[VMEM] * 6,
        out_specs=[VMEM] * 2,
        out_shape=[
            jax.ShapeDtypeStruct((rows, 2 * (width + EXPERTS)), BF16),
            jax.ShapeDtypeStruct((keys.shape[0], 2 * keys.shape[1]), BF16),
        ],
        name="pack",
    )(ids, gates, x, grad, keys, values)


def attention_kernel(base_ref, q_ref, *refs):
    out_ref = refs[-1]
    kv_refs = refs[:-1]
    rows, width = q_ref.shape
    half = kv_refs[0].shape[1] // 2
    kv_heads = half // HD
    repeat = width // HD // kv_heads
    scale = math.log2(math.e) / HD**0.5
    row_pos = base_ref[0] * rows + lax.broadcasted_iota(jnp.int32, (rows, rows), 0)
    col_pos = lax.broadcasted_iota(jnp.int32, (rows, rows), 1)
    masks = [
        jnp.where(col_pos + base_ref[p] * rows <= row_pos, 0.0, -jnp.inf)
        for p in range(len(kv_refs))
    ]
    bias = jnp.concatenate(masks, axis=1)
    for g in range(kv_heads):
        keys = jnp.concatenate([r[:, g * HD : (g + 1) * HD] for r in kv_refs], axis=0)
        vals = jnp.concatenate(
            [r[:, half + g * HD : half + (g + 1) * HD] for r in kv_refs], axis=0
        )
        vals = jnp.concatenate([vals, jnp.ones_like(vals)], axis=1)
        for h in range(g * repeat, (g + 1) * repeat):
            cols = slice(h * HD, (h + 1) * HD)
            scores = lax.dot_general(q_ref[:, cols], keys, NT, preferred_element_type=F32) + bias
            top = jnp.max(scores, axis=1, keepdims=True)
            probs = jnp.exp2((scores - top) * scale).astype(BF16)
            mixed = jnp.dot(probs, vals, preferred_element_type=F32)
            out_ref[:, cols] = (mixed[:, :HD] / mixed[:, HD:]).astype(BF16)


def attend(base, q, kv):
    rows, width = q.shape
    keys = rows * len(kv)
    return pl.pallas_call(
        attention_kernel,
        in_specs=[SMEM] + [VMEM] * (1 + len(kv)),
        out_specs=VMEM,
        out_shape=jax.ShapeDtypeStruct((rows, width), BF16),
        cost_estimate=pl.CostEstimate(
            flops=4 * rows * keys * width, bytes_accessed=4 * rows * width, transcendentals=0
        ),
        name="attention",
    )(base, q, *kv)


def routing_rows(shard, gates, local, slots):
    tokens, lanes = gates.shape
    lane = lax.broadcasted_iota(jnp.int32, (local, lanes), 1)
    mine = shard * local + lax.broadcasted_iota(jnp.int32, (local, lanes), 0)
    columns = ((lane == mine) | (lane == mine + EXPERTS)).astype(BF16)
    weight = lax.dot_general(columns, gates, NT, preferred_element_type=F32)
    live = weight > 0
    earlier = lax.broadcasted_iota(jnp.int32, (tokens, tokens), 0)
    earlier = (earlier < lax.broadcasted_iota(jnp.int32, (tokens, tokens), 1)).astype(BF16)
    rank = jnp.dot(live.astype(BF16), earlier, preferred_element_type=F32)
    slot = lax.broadcasted_iota(jnp.int32, (slots, tokens), 0).astype(F32)
    picks, scales = [], []
    for e in range(local):
        pick = jnp.where((slot == rank[e : e + 1]) & live[e : e + 1], 1.0, 0.0)
        picks.append(pick)
        scales.append(jnp.sum(pick * weight[e : e + 1], axis=1, keepdims=True))
    return jnp.concatenate(picks, axis=0), jnp.concatenate(scales, axis=0)


def experts_kernel(shard_ref, *refs, count, slots):
    pieces = refs[:count]
    weights = refs[count : count + 3]
    outs = refs[count + 3 : 2 * count + 3]
    held, sems, tokens_scr, rows_scr, back_scr, scale_scr, pick_scr = refs[2 * count + 3 :]
    gate_scr, up_scr, down_scr = held
    local, width, hidden = gate_scr.shape
    piece = pieces[0].shape[0]
    both = 2 * width

    def copy(which, e):
        return pltpu.make_async_copy(
            weights[which].at[e], held[which].at[e], sems.at[which, e]
        )

    for e in range(local):
        for which in range(3):
            copy(which, e).start()

    for p in range(count):
        tokens_scr[p * piece : (p + 1) * piece] = pieces[p][:, :both]
    gates = jnp.concatenate([r[:, both:] for r in pieces], axis=0)
    picks, scales = routing_rows(shard_ref[0], gates, local, slots)
    scale_scr[...] = jnp.broadcast_to(scales, scale_scr.shape)
    high = scales.astype(BF16).astype(F32)
    for i, part in enumerate((picks, picks * high, picks * (scales - high))):
        pick_scr[i] = jnp.transpose(part).astype(BF16)
    picks = picks.astype(BF16)
    chunk = 512
    for c in range(0, both, chunk):
        rows_scr[:, c : c + chunk] = jnp.dot(
            picks, tokens_scr[:, c : c + chunk], preferred_element_type=F32
        ).astype(BF16)

    unroll = 2 if local % 2 == 0 else 1

    @pl.loop(0, local // unroll)
    def _(step):
        state = []
        for k in range(unroll):
            e = step * unroll + k
            for which in range(3):
                copy(which, e).wait()
        for k in range(unroll):
            e = step * unroll + k
            mine = pl.ds(pl.multiple_of(e * slots, slots), slots)
            entry = jnp.concatenate([gate_scr[e], up_scr[e]], axis=1)
            hidden_both = jnp.dot(rows_scr[mine, :width], entry, preferred_element_type=F32)
            row_grad = (rows_scr[mine, width:].astype(F32) * scale_scr[mine, :1]).astype(BF16)
            grad_act = lax.dot_general(row_grad, down_scr[e], NT, preferred_element_type=F32)
            state.append((hidden_both, grad_act))
        for k in range(unroll):
            e = step * unroll + k
            mine = pl.ds(pl.multiple_of(e * slots, slots), slots)
            hidden_both, grad_act = state[k]
            hgate, hup = hidden_both[:, :hidden], hidden_both[:, hidden:]
            sig = jax.nn.sigmoid(hgate)
            silu = hgate * sig
            activated = (silu * hup).astype(BF16)
            grad_gate = (grad_act * hup * sig * (1.0 + hgate * (1.0 - sig))).astype(BF16)
            grad_up = (grad_act * silu).astype(BF16)
            back_scr[mine, :width] = jnp.dot(
                activated, down_scr[e], preferred_element_type=F32
            ).astype(BF16)
            grads = jnp.concatenate([grad_gate, grad_up], axis=1)
            entry = jnp.concatenate([gate_scr[e], up_scr[e]], axis=1)
            back_scr[mine, width:] = lax.dot_general(
                grads, entry, NT, preferred_element_type=F32
            ).astype(BF16)

    for c in range(0, both, chunk):
        rows = back_scr[:, c : c + chunk]
        if c < width:
            total = jnp.dot(pick_scr[1], rows, preferred_element_type=F32)
            total = total + jnp.dot(pick_scr[2], rows, preferred_element_type=F32)
        else:
            total = jnp.dot(pick_scr[0], rows, preferred_element_type=F32)
        total = total.astype(BF16)
        for p in range(count):
            outs[p][:, c : c + chunk] = total[p * piece : (p + 1) * piece]


def experts(shard, pieces, w_gate, w_up, w_down):
    count = len(pieces)
    local, width, hidden = w_gate.shape
    piece = pieces[0].shape[0]
    tokens = count * piece
    slots = -(-CAP * count // 16) * 16
    scratch = [
        tuple(pltpu.VMEM(w.shape, BF16) for w in (w_gate, w_up, w_down)),
        pltpu.SemaphoreType.DMA((3, local)),
        pltpu.VMEM((tokens, 2 * width), BF16),
        pltpu.VMEM((local * slots, 2 * width), BF16),
        pltpu.VMEM((local * slots, 2 * width), BF16),
        pltpu.VMEM((local * slots, 128), F32),
        pltpu.VMEM((3, tokens, local * slots), BF16),
    ]
    held_bytes = 6 * local * width * hidden + 4 * width * (tokens + 2 * local * slots)
    return pl.pallas_call(
        functools.partial(experts_kernel, count=count, slots=slots),
        in_specs=[SMEM] + [VMEM] * count + [pl.BlockSpec(memory_space=pl.ANY)] * 3,
        out_specs=[VMEM] * count,
        out_shape=[jax.ShapeDtypeStruct((piece, 2 * width), BF16)] * count,
        scratch_shapes=scratch,
        compiler_params=pltpu.CompilerParams(vmem_limit_bytes=held_bytes + 10 * 2**20),
        cost_estimate=pl.CostEstimate(
            flops=12 * local * slots * width * hidden,
            bytes_accessed=6 * local * width * hidden,
            transcendentals=0,
        ),
        name="experts",
    )(shard, *pieces, w_gate, w_up, w_down)


def parent(offset):
    return offset & (offset - 1)


def spread(rows, held):
    near, far = [rows], []
    for d in range(1, lax.axis_size("seq")):
        block = swap(near[parent(d)], "seq", d - parent(d))
        far.append([swap(near[d - 1], "tp", t) for t in range(1, lax.axis_size("tp"))])
        if d > 1:
            block, far[d - 2] = lax.optimization_barrier((block, far[d - 2]))
        near.append(block)
    far.append([swap(near[-1], "tp", t) for t in range(1, lax.axis_size("tp"))])
    near[-1], result = held(near[-1])
    return near + [a for blocks in zip(*far) for a in blocks], result


def collect(pieces):
    seq, tp = lax.axis_size("seq"), lax.axis_size("tp")
    terms = [[pieces[d]] for d in range(seq)]
    for d in reversed(range(seq)):
        terms[d] += [swap(pieces[t * seq + d], "tp", t) for t in range(1, tp)]
        total = sum(a.astype(F32) for a in terms[d]).astype(BF16)
        if d:
            terms[d] = []
            terms[parent(d)].append(swap(total, "seq", d - parent(d)))
        if d and d % 8 == 0:
            pieces, terms = lax.optimization_barrier((pieces, terms))
    return total


def shards(queries, keys, values, moe_x, expert_ids, gates, grad_out, w_gate, w_up, w_down):
    group = lax.axis_index("group")
    shard = (lax.axis_index("seq") * lax.axis_size("tp") + lax.axis_index("tp")).reshape(1)
    rows, kv = pack(expert_ids[0].T, gates[0].T, moe_x[0], grad_out[0], keys[0], values[0])
    offsets = range(lax.axis_size("group"))
    kv_pieces = [kv] + [swap(kv, "group", d) for d in offsets[1:]]
    base = jnp.stack([group ^ d for d in offsets])

    def attended(block):
        block, starts = lax.optimization_barrier((block, base))
        return block, attend(starts, queries[0], kv_pieces)

    pieces, attn_out = spread(rows, attended)
    pieces, attn_out = lax.optimization_barrier((pieces, attn_out))
    total = collect(experts(shard, pieces, w_gate, w_up, w_down))
    width = moe_x.shape[-1]
    return attn_out[None], total[None, :, :width], total[None, :, width:]


def solution(mesh):
    rows = P("seq", "group", "tp")
    tokens = P("group", ("seq", "tp"), None)
    experts = P(("seq", "tp"), None, None)
    return jax.shard_map(
        shards,
        mesh=mesh,
        in_specs=(rows, rows, rows, tokens, tokens, tokens, tokens, experts, experts, experts),
        out_specs=(rows, tokens, tokens),
        check_vma=False,
    )
```

```python
import functools
import math

import jax
import jax.numpy as jnp
from jax import lax
from jax.experimental import pallas as pl
from jax.experimental.pallas import tpu as pltpu
from jax.sharding import PartitionSpec as P

H = 32
KVH = 4
HD = 128
EXPERTS = 64
CAP = 3
NT = (((1,), (1,)), ((), ()))
VMEM = pl.BlockSpec(memory_space=pltpu.VMEM)
SMEM = pl.BlockSpec(memory_space=pltpu.SMEM)
F32 = jnp.float32
BF16 = jnp.bfloat16


def swap(array, axis, offset):
    count = lax.axis_size(axis)
    return lax.ppermute(array, axis, [(i, i ^ offset) for i in range(count)])


def pack_kernel(ids_ref, gates_ref, x_ref, grad_ref, key_ref, value_ref, out_ref, kv_ref):
    rows, width = x_ref.shape
    topk = ids_ref.shape[0]
    expert = lax.broadcasted_iota(jnp.int32, (EXPERTS, rows), 0)
    table = jnp.zeros((EXPERTS, rows), F32)
    for k in range(topk):
        table = table + jnp.where(ids_ref[k : k + 1] == expert, gates_ref[k : k + 1], 0.0)
    high = table.astype(BF16).astype(F32)
    both = jnp.concatenate([high, table - high], axis=0)
    out_ref[:, :width] = x_ref[...]
    out_ref[:, width : 2 * width] = grad_ref[...]
    out_ref[:, 2 * width :] = jnp.transpose(both).astype(BF16)
    half = key_ref.shape[1]
    kv_ref[:, :half] = key_ref[...]
    kv_ref[:, half:] = value_ref[...]


def pack(ids, gates, x, grad, keys, values):
    rows, width = x.shape
    return pl.pallas_call(
        pack_kernel,
        in_specs=[VMEM] * 6,
        out_specs=[VMEM] * 2,
        out_shape=[
            jax.ShapeDtypeStruct((rows, 2 * (width + EXPERTS)), BF16),
            jax.ShapeDtypeStruct((keys.shape[0], 2 * keys.shape[1]), BF16),
        ],
        name="pack",
    )(ids, gates, x, grad, keys, values)


def attention_kernel(base_ref, q_ref, *refs):
    out_ref = refs[-1]
    kv_refs = refs[:-1]
    rows, width = q_ref.shape
    half = kv_refs[0].shape[1] // 2
    kv_heads = half // HD
    repeat = width // HD // kv_heads
    scale = math.log2(math.e) / HD**0.5
    row_pos = base_ref[0] * rows + lax.broadcasted_iota(jnp.int32, (rows, rows), 0)
    col_pos = lax.broadcasted_iota(jnp.int32, (rows, rows), 1)
    masks = [
        jnp.where(col_pos + base_ref[p] * rows <= row_pos, 0.0, -jnp.inf)
        for p in range(len(kv_refs))
    ]
    bias = jnp.concatenate(masks, axis=1)
    for g in range(kv_heads):
        keys = jnp.concatenate([r[:, g * HD : (g + 1) * HD] for r in kv_refs], axis=0)
        vals = jnp.concatenate(
            [r[:, half + g * HD : half + (g + 1) * HD] for r in kv_refs], axis=0
        )
        vals = jnp.concatenate([vals, jnp.ones_like(vals)], axis=1)
        for h in range(g * repeat, (g + 1) * repeat):
            cols = slice(h * HD, (h + 1) * HD)
            scores = lax.dot_general(q_ref[:, cols], keys, NT, preferred_element_type=F32) + bias
            top = jnp.max(scores, axis=1, keepdims=True)
            probs = jnp.exp2((scores - top) * scale).astype(BF16)
            mixed = jnp.dot(probs, vals, preferred_element_type=F32)
            out_ref[:, cols] = (mixed[:, :HD] / mixed[:, HD:]).astype(BF16)


def attend(base, q, kv):
    rows, width = q.shape
    keys = rows * len(kv)
    return pl.pallas_call(
        attention_kernel,
        in_specs=[SMEM] + [VMEM] * (1 + len(kv)),
        out_specs=VMEM,
        out_shape=jax.ShapeDtypeStruct((rows, width), BF16),
        cost_estimate=pl.CostEstimate(
            flops=4 * rows * keys * width, bytes_accessed=4 * rows * width, transcendentals=0
        ),
        name="attention",
    )(base, q, *kv)


def routing_rows(shard, gates, local, slots):
    tokens, lanes = gates.shape
    lane = lax.broadcasted_iota(jnp.int32, (local, lanes), 1)
    mine = shard * local + lax.broadcasted_iota(jnp.int32, (local, lanes), 0)
    columns = ((lane == mine) | (lane == mine + EXPERTS)).astype(BF16)
    weight = lax.dot_general(columns, gates, NT, preferred_element_type=F32)
    live = weight > 0
    earlier = lax.broadcasted_iota(jnp.int32, (tokens, tokens), 0)
    earlier = (earlier < lax.broadcasted_iota(jnp.int32, (tokens, tokens), 1)).astype(BF16)
    rank = jnp.dot(live.astype(BF16), earlier, preferred_element_type=F32)
    slot = lax.broadcasted_iota(jnp.int32, (slots, tokens), 0).astype(F32)
    picks, scales = [], []
    for e in range(local):
        pick = jnp.where((slot == rank[e : e + 1]) & live[e : e + 1], 1.0, 0.0)
        picks.append(pick)
        scales.append(jnp.sum(pick * weight[e : e + 1], axis=1, keepdims=True))
    return jnp.concatenate(picks, axis=0), jnp.concatenate(scales, axis=0)


def experts_kernel(shard_ref, *refs, count, slots):
    pieces = refs[:count]
    weights = refs[count : count + 3]
    outs = refs[count + 3 : 2 * count + 3]
    held, sems, tokens_scr, rows_scr, back_scr, scale_scr, pick_scr = refs[2 * count + 3 :]
    gate_scr, up_scr, down_scr = held
    local, width, hidden = gate_scr.shape
    piece = pieces[0].shape[0]
    both = 2 * width

    def copy(which, e):
        return pltpu.make_async_copy(
            weights[which].at[e], held[which].at[e], sems.at[which, e]
        )

    for e in range(local):
        for which in range(3):
            copy(which, e).start()

    for p in range(count):
        tokens_scr[p * piece : (p + 1) * piece] = pieces[p][:, :both]
    gates = jnp.concatenate([r[:, both:] for r in pieces], axis=0)
    picks, scales = routing_rows(shard_ref[0], gates, local, slots)
    scale_scr[...] = jnp.broadcast_to(scales, scale_scr.shape)
    high = scales.astype(BF16).astype(F32)
    for i, part in enumerate((picks, picks * high, picks * (scales - high))):
        pick_scr[i] = jnp.transpose(part).astype(BF16)
    picks = picks.astype(BF16)
    chunk = 512
    for c in range(0, both, chunk):
        rows_scr[:, c : c + chunk] = jnp.dot(
            picks, tokens_scr[:, c : c + chunk], preferred_element_type=F32
        ).astype(BF16)

    unroll = 2 if local % 2 == 0 else 1

    @pl.loop(0, local // unroll)
    def _(step):
        state = []
        for k in range(unroll):
            e = step * unroll + k
            for which in range(3):
                copy(which, e).wait()
        for k in range(unroll):
            e = step * unroll + k
            mine = pl.ds(pl.multiple_of(e * slots, slots), slots)
            entry = jnp.concatenate([gate_scr[e], up_scr[e]], axis=1)
            hidden_both = jnp.dot(rows_scr[mine, :width], entry, preferred_element_type=F32)
            row_grad = (rows_scr[mine, width:].astype(F32) * scale_scr[mine, :1]).astype(BF16)
            grad_act = lax.dot_general(row_grad, down_scr[e], NT, preferred_element_type=F32)
            state.append((hidden_both, grad_act))
        for k in range(unroll):
            e = step * unroll + k
            mine = pl.ds(pl.multiple_of(e * slots, slots), slots)
            hidden_both, grad_act = state[k]
            hgate, hup = hidden_both[:, :hidden], hidden_both[:, hidden:]
            sig = jax.nn.sigmoid(hgate)
            silu = hgate * sig
            activated = (silu * hup).astype(BF16)
            grad_gate = (grad_act * hup * sig * (1.0 + hgate * (1.0 - sig))).astype(BF16)
            grad_up = (grad_act * silu).astype(BF16)
            back_scr[mine, :width] = jnp.dot(
                activated, down_scr[e], preferred_element_type=F32
            ).astype(BF16)
            grads = jnp.concatenate([grad_gate, grad_up], axis=1)
            entry = jnp.concatenate([gate_scr[e], up_scr[e]], axis=1)
            back_scr[mine, width:] = lax.dot_general(
                grads, entry, NT, preferred_element_type=F32
            ).astype(BF16)

    for c in range(0, both, chunk):
        rows = back_scr[:, c : c + chunk]
        if c < width:
            total = jnp.dot(pick_scr[1], rows, preferred_element_type=F32)
            total = total + jnp.dot(pick_scr[2], rows, preferred_element_type=F32)
        else:
            total = jnp.dot(pick_scr[0], rows, preferred_element_type=F32)
        total = total.astype(BF16)
        for p in range(count):
            outs[p][:, c : c + chunk] = total[p * piece : (p + 1) * piece]


def experts(shard, pieces, w_gate, w_up, w_down):
    count = len(pieces)
    local, width, hidden = w_gate.shape
    piece = pieces[0].shape[0]
    tokens = count * piece
    slots = -(-CAP * count // 16) * 16
    scratch = [
        tuple(pltpu.VMEM(w.shape, BF16) for w in (w_gate, w_up, w_down)),
        pltpu.SemaphoreType.DMA((3, local)),
        pltpu.VMEM((tokens, 2 * width), BF16),
        pltpu.VMEM((local * slots, 2 * width), BF16),
        pltpu.VMEM((local * slots, 2 * width), BF16),
        pltpu.VMEM((local * slots, 128), F32),
        pltpu.VMEM((3, tokens, local * slots), BF16),
    ]
    held_bytes = 6 * local * width * hidden + 4 * width * (tokens + 2 * local * slots)
    return pl.pallas_call(
        functools.partial(experts_kernel, count=count, slots=slots),
        in_specs=[SMEM] + [VMEM] * count + [pl.BlockSpec(memory_space=pl.ANY)] * 3,
        out_specs=[VMEM] * count,
        out_shape=[jax.ShapeDtypeStruct((piece, 2 * width), BF16)] * count,
        scratch_shapes=scratch,
        compiler_params=pltpu.CompilerParams(vmem_limit_bytes=held_bytes + 10 * 2**20),
        cost_estimate=pl.CostEstimate(
            flops=12 * local * slots * width * hidden,
            bytes_accessed=6 * local * width * hidden,
            transcendentals=0,
        ),
        name="experts",
    )(shard, *pieces, w_gate, w_up, w_down)


def parent(offset):
    return offset & (offset - 1)


def spread(rows, kv):
    near, far = [rows], []
    kv_pieces, offsets = [kv], [0]
    step = lax.axis_size("group") // 2
    for d in range(1, lax.axis_size("seq")):
        block = swap(near[parent(d)], "seq", d - parent(d))
        far.append([swap(near[d - 1], "tp", t) for t in range(1, lax.axis_size("tp"))])
        if d > 1:
            if step:
                kv_pieces = kv_pieces + [swap(a, "group", step) for a in kv_pieces]
                offsets = offsets + [o ^ step for o in offsets]
                step //= 2
            block, far[d - 2], kv_pieces = lax.optimization_barrier((block, far[d - 2], kv_pieces))
        near.append(block)
    while step:
        kv_pieces = kv_pieces + [swap(a, "group", step) for a in kv_pieces]
        offsets = offsets + [o ^ step for o in offsets]
        step //= 2
    far.append([swap(near[-1], "tp", t) for t in range(1, lax.axis_size("tp"))])
    return near + [a for blocks in zip(*far) for a in blocks], kv_pieces, offsets


def collect(pieces, beside):
    seq, tp = lax.axis_size("seq"), lax.axis_size("tp")
    terms = [[pieces[d]] for d in range(seq)]
    order = sorted(range(seq), key=lambda d: (-d.bit_count(), d))
    last = None
    for d in order:
        terms[d] += [swap(pieces[t * seq + d], "tp", t) for t in range(1, tp)]
        if d == 0:
            break
        if last is not None:
            _, terms[d] = lax.optimization_barrier((last, terms[d]))
        last = sum(a.astype(F32) for a in terms[d]).astype(BF16)
        terms[parent(d)].append(swap(last, "seq", d - parent(d)))
    result = beside(last)
    terms[0], result = lax.optimization_barrier((terms[0], result))
    return sum(a.astype(F32) for a in terms[0]).astype(BF16), result


def shards(queries, keys, values, moe_x, expert_ids, gates, grad_out, w_gate, w_up, w_down):
    group = lax.axis_index("group")
    shard = (lax.axis_index("seq") * lax.axis_size("tp") + lax.axis_index("tp")).reshape(1)
    rows, kv = pack(expert_ids[0].T, gates[0].T, moe_x[0], grad_out[0], keys[0], values[0])
    pieces, kv_pieces, offsets = spread(rows, kv)
    base = jnp.stack([group ^ d for d in offsets])

    def attended(sums):
        _, first = lax.optimization_barrier((sums, kv_pieces[0]))
        return attend(base, queries[0], [first] + kv_pieces[1:])

    partial = experts(shard, pieces, w_gate, w_up, w_down)
    total, attn_out = collect(partial, attended)
    width = moe_x.shape[-1]
    return attn_out[None], total[None, :, :width], total[None, :, width:]


def solution(mesh):
    rows = P("seq", "group", "tp")
    tokens = P("group", ("seq", "tp"), None)
    experts = P(("seq", "tp"), None, None)
    return jax.shard_map(
        shards,
        mesh=mesh,
        in_specs=(rows, rows, rows, tokens, tokens, tokens, tokens, experts, experts, experts),
        out_specs=(rows, tokens, tokens),
        check_vma=False,
    )
```

```python
import functools
import math

import jax
import jax.numpy as jnp
from jax import lax
from jax.experimental import pallas as pl
from jax.experimental.pallas import tpu as pltpu
from jax.sharding import PartitionSpec as P

H = 32
KVH = 4
HD = 128
EXPERTS = 64
CAP = 3
NT = (((1,), (1,)), ((), ()))
VMEM = pl.BlockSpec(memory_space=pltpu.VMEM)
SMEM = pl.BlockSpec(memory_space=pltpu.SMEM)
ANY = pl.BlockSpec(memory_space=pl.ANY)
F32 = jnp.float32
BF16 = jnp.bfloat16


def swap(array, axis, offset):
    count = lax.axis_size(axis)
    return lax.ppermute(array, axis, [(i, i ^ offset) for i in range(count)])


def pack_kernel(ids_ref, gates_ref, x_ref, grad_ref, out_ref, own_ref):
    rows, width = x_ref.shape
    topk = ids_ref.shape[0]
    expert = lax.broadcasted_iota(jnp.int32, (EXPERTS, rows), 0)
    table = jnp.zeros((EXPERTS, rows), F32)
    for k in range(topk):
        table = table + jnp.where(ids_ref[k : k + 1] == expert, gates_ref[k : k + 1], 0.0)
    high = table.astype(BF16).astype(F32)
    both = jnp.concatenate([high, table - high], axis=0)
    both = jnp.transpose(both).astype(BF16)
    for ref in (out_ref, own_ref):
        ref[:, :width] = x_ref[...]
        ref[:, width : 2 * width] = grad_ref[...]
        ref[:, 2 * width :] = both


def pack_rows(ids, gates, x, grad):
    rows, width = x.shape
    return pl.pallas_call(
        pack_kernel,
        in_specs=[VMEM] * 4,
        out_specs=[VMEM] * 2,
        out_shape=[
            jax.ShapeDtypeStruct((rows, 2 * (width + EXPERTS)), BF16),
            pltpu.VMEM((rows, 2 * (width + EXPERTS)), BF16),
        ],
        name="pack_rows",
    )(ids, gates, x, grad)


def attention_kernel(base_ref, q_ref, *refs):
    out_ref = refs[-1]
    kv_refs = refs[:-1]
    rows, width = q_ref.shape
    half = kv_refs[0].shape[1] // 2
    kv_heads = half // HD
    repeat = width // HD // kv_heads
    scale = math.log2(math.e) / HD**0.5
    row_pos = base_ref[0] * rows + lax.broadcasted_iota(jnp.int32, (rows, rows), 0)
    col_pos = lax.broadcasted_iota(jnp.int32, (rows, rows), 1)
    masks = [
        jnp.where(col_pos + base_ref[p] * rows <= row_pos, 0.0, -jnp.inf)
        for p in range(len(kv_refs))
    ]
    bias = jnp.concatenate(masks, axis=1)
    for g in range(kv_heads):
        keys = jnp.concatenate([r[:, g * HD : (g + 1) * HD] for r in kv_refs], axis=0)
        vals = jnp.concatenate(
            [r[:, half + g * HD : half + (g + 1) * HD] for r in kv_refs], axis=0
        )
        vals = jnp.concatenate([vals, jnp.ones_like(vals)], axis=1)
        for h in range(g * repeat, (g + 1) * repeat):
            cols = slice(h * HD, (h + 1) * HD)
            scores = lax.dot_general(q_ref[:, cols], keys, NT, preferred_element_type=F32) + bias
            top = jnp.max(scores, axis=1, keepdims=True)
            probs = jnp.exp2((scores - top) * scale).astype(BF16)
            mixed = jnp.dot(probs, vals, preferred_element_type=F32)
            out_ref[:, cols] = (mixed[:, :HD] / mixed[:, HD:]).astype(BF16)


def attend(base, q, kv):
    rows, width = q.shape
    keys = rows * len(kv)
    return pl.pallas_call(
        attention_kernel,
        in_specs=[SMEM] + [VMEM] * (1 + len(kv)),
        out_specs=VMEM,
        out_shape=jax.ShapeDtypeStruct((rows, width), BF16),
        cost_estimate=pl.CostEstimate(
            flops=4 * rows * keys * width, bytes_accessed=4 * rows * width, transcendentals=0
        ),
        name="attention",
    )(base, q, *kv)


def routing_rows(shard, gates, local, slots):
    tokens, lanes = gates.shape
    lane = lax.broadcasted_iota(jnp.int32, (local, lanes), 1)
    mine = shard * local + lax.broadcasted_iota(jnp.int32, (local, lanes), 0)
    columns = ((lane == mine) | (lane == mine + EXPERTS)).astype(BF16)
    weight = lax.dot_general(columns, gates, NT, preferred_element_type=F32)
    live = weight > 0
    earlier = lax.broadcasted_iota(jnp.int32, (tokens, tokens), 0)
    earlier = (earlier < lax.broadcasted_iota(jnp.int32, (tokens, tokens), 1)).astype(BF16)
    rank = jnp.dot(live.astype(BF16), earlier, preferred_element_type=F32)
    slot = lax.broadcasted_iota(jnp.int32, (slots, tokens), 0).astype(F32)
    picks, scales = [], []
    for e in range(local):
        pick = jnp.where((slot == rank[e : e + 1]) & live[e : e + 1], 1.0, 0.0)
        picks.append(pick)
        scales.append(jnp.sum(pick * weight[e : e + 1], axis=1, keepdims=True))
    return jnp.concatenate(picks, axis=0), jnp.concatenate(scales, axis=0)


def experts_kernel(shard_ref, *refs, count, slots):
    pieces = refs[:count]
    weights = refs[count : count + 3]
    outs = refs[count + 3 : 2 * count + 3]
    held, sems, tokens_scr, gates_scr, rows_scr, back_scr, scale_scr, pick_scr = refs[
        2 * count + 3 :
    ]
    gate_scr, up_scr, down_scr = held
    local, width, hidden = gate_scr.shape
    piece = pieces[0].shape[0]
    both = 2 * width

    def copy(which, e):
        return pltpu.make_async_copy(
            weights[which].at[e], held[which].at[e], sems.at[which, e]
        )

    for e in range(local):
        for which in range(3):
            copy(which, e).start()

    for p in range(count):
        tokens_scr[p * piece : (p + 1) * piece] = pieces[p][:, :both]
        gates_scr[p * piece : (p + 1) * piece] = pieces[p][:, both:]
    picks, scales = routing_rows(shard_ref[0], gates_scr[...], local, slots)
    scale_scr[...] = jnp.broadcast_to(scales, scale_scr.shape)
    high = scales.astype(BF16).astype(F32)
    for i, part in enumerate((picks, picks * high, picks * (scales - high))):
        pick_scr[i] = jnp.transpose(part).astype(BF16)
    picks = picks.astype(BF16)
    chunk = 512
    for c in range(0, both, chunk):
        rows_scr[:, c : c + chunk] = jnp.dot(
            picks, tokens_scr[:, c : c + chunk], preferred_element_type=F32
        ).astype(BF16)

    unroll = 2 if local % 2 == 0 else 1

    @pl.loop(0, local // unroll)
    def _(step):
        first = step * unroll
        for k in range(unroll):
            for which in range(3):
                copy(which, first + k).wait()
        every = pl.ds(pl.multiple_of(first * slots, slots), unroll * slots)
        down = down_scr.at[pl.ds(first, unroll)].reshape(unroll * hidden, width)
        row_grad = (rows_scr[every, width:].astype(F32) * scale_scr[every, :1]).astype(BF16)
        hidden_both, mine = [], []
        for k in range(unroll):
            mine.append(pl.ds(pl.multiple_of((first + k) * slots, slots), slots))
            entry = jnp.concatenate([gate_scr[first + k], up_scr[first + k]], axis=1)
            hidden_both.append(jnp.dot(rows_scr[mine[k], :width], entry, preferred_element_type=F32))
        grad_act = lax.dot_general(row_grad, down[...], NT, preferred_element_type=F32)
        activated = []
        for k in range(unroll):
            part = grad_act[k * slots : (k + 1) * slots, k * hidden : (k + 1) * hidden]
            hgate, hup = hidden_both[k][:, :hidden], hidden_both[k][:, hidden:]
            sig = jax.nn.sigmoid(hgate)
            silu = hgate * sig
            activated.append((silu * hup).astype(BF16))
            grad_gate = (part * hup * sig * (1.0 + hgate * (1.0 - sig))).astype(BF16)
            grad_up = (part * silu).astype(BF16)
            grads = jnp.concatenate([grad_gate, grad_up], axis=1)
            entry = jnp.concatenate([gate_scr[first + k], up_scr[first + k]], axis=1)
            back_scr[mine[k], width:] = lax.dot_general(
                grads, entry, NT, preferred_element_type=F32
            ).astype(BF16)
        blocks = [
            jnp.concatenate(
                [a if k == i else jnp.zeros_like(a) for i in range(unroll)], axis=1
            )
            for k, a in enumerate(activated)
        ]
        back_scr[every, :width] = jnp.dot(
            jnp.concatenate(blocks, axis=0), down[...], preferred_element_type=F32
        ).astype(BF16)

    for c in range(0, both, chunk):
        rows = back_scr[:, c : c + chunk]
        if c < width:
            total = jnp.dot(pick_scr[1], rows, preferred_element_type=F32)
            total = total + jnp.dot(pick_scr[2], rows, preferred_element_type=F32)
        else:
            total = jnp.dot(pick_scr[0], rows, preferred_element_type=F32)
        total = total.astype(BF16)
        for p in range(count):
            outs[p][:, c : c + chunk] = total[p * piece : (p + 1) * piece]


def experts(shard, pieces, w_gate, w_up, w_down):
    count = len(pieces)
    pieces = [pltpu.with_memory_space_constraint(pieces[0], pltpu.VMEM)] + pieces[1:]
    local, width, hidden = w_gate.shape
    piece = pieces[0].shape[0]
    tokens = count * piece
    slots = -(-CAP * count // 16) * 16
    scratch = [
        tuple(pltpu.VMEM(w.shape, BF16) for w in (w_gate, w_up, w_down)),
        pltpu.SemaphoreType.DMA((3, local)),
        pltpu.VMEM((tokens, 2 * width), BF16),
        pltpu.VMEM((tokens, pieces[0].shape[1] - 2 * width), BF16),
        pltpu.VMEM((local * slots, 2 * width), BF16),
        pltpu.VMEM((local * slots, 2 * width), BF16),
        pltpu.VMEM((local * slots, 128), F32),
        pltpu.VMEM((3, tokens, local * slots), BF16),
    ]
    held_bytes = 6 * local * width * hidden + 4 * width * (tokens + 2 * local * slots)
    return pl.pallas_call(
        functools.partial(experts_kernel, count=count, slots=slots),
        in_specs=[SMEM] + [VMEM] * count + [ANY] * 3,
        out_specs=[VMEM] * count,
        out_shape=[jax.ShapeDtypeStruct((piece, 2 * width), BF16)] * count,
        scratch_shapes=scratch,
        compiler_params=pltpu.CompilerParams(vmem_limit_bytes=held_bytes + 10 * 2**20),
        cost_estimate=pl.CostEstimate(
            flops=12 * local * slots * width * hidden,
            bytes_accessed=6 * local * width * hidden,
            transcendentals=0,
        ),
        name="experts",
    )(shard, *pieces, w_gate, w_up, w_down)


def parent(offset):
    return offset & (offset - 1)


def over_tp(block):
    return [swap(block, "tp", t) for t in range(1, lax.axis_size("tp"))]


def spread(rows):
    near, far = [rows], []
    for d in range(1, lax.axis_size("seq")):
        block = swap(near[parent(d)], "seq", d - parent(d))
        if d == 1:
            block, rows = lax.optimization_barrier((block, rows))
            far.append(over_tp(rows))
        else:
            far.append(over_tp(near[d - 1]))
        if d > 2:
            block, far[: d - 1] = lax.optimization_barrier((block, far[: d - 1]))
        near.append(block)
    far.append(over_tp(near[-1]))
    return near + [a for blocks in zip(*far) for a in blocks]


def collect(pieces, kv, beside):
    seq, tp = lax.axis_size("seq"), lax.axis_size("tp")
    terms = [[pieces[d]] for d in range(seq)]
    order = sorted(range(seq), key=lambda d: (-d.bit_count(), d))
    step = lax.axis_size("group") // 2
    kv, offsets = [kv], [0]
    last = None
    for d in order:
        terms[d] += [swap(pieces[t * seq + d], "tp", t) for t in range(1, tp)]
        if d == 0:
            break
        if last is not None:
            if step:
                kv = kv + [swap(a, "group", step) for a in kv]
                offsets = offsets + [o ^ step for o in offsets]
                step //= 2
            _, terms[d], kv = lax.optimization_barrier((last, terms[d], kv))
        last = sum(a.astype(F32) for a in terms[d]).astype(BF16)
        terms[parent(d)].append(swap(last, "seq", d - parent(d)))
    while step:
        kv = kv + [swap(a, "group", step) for a in kv]
        offsets = offsets + [o ^ step for o in offsets]
        step //= 2
    result = beside(last, kv, offsets)
    terms[0], result = lax.optimization_barrier((terms[0], result))
    return sum(a.astype(F32) for a in terms[0]).astype(BF16), result


def shards(queries, keys, values, moe_x, expert_ids, gates, grad_out, w_gate, w_up, w_down):
    group = lax.axis_index("group")
    shard = (lax.axis_index("seq") * lax.axis_size("tp") + lax.axis_index("tp")).reshape(1)
    rows, own = pack_rows(expert_ids[0].T, gates[0].T, moe_x[0], grad_out[0])
    pieces = spread(rows)
    _, *kv = lax.optimization_barrier((pieces[1], keys[0], values[0]))
    kv = jnp.concatenate(kv, axis=1)
    pieces[2:], kv = lax.optimization_barrier((pieces[2:], kv))
    partial = experts(shard, [own] + pieces[1:], w_gate, w_up, w_down)
    partial, kv = lax.optimization_barrier((partial, kv))

    def attended(sums, kv_pieces, offsets):
        _, first = lax.optimization_barrier((sums, kv_pieces[0]))
        base = jnp.stack([group ^ d for d in offsets])
        return attend(base, queries[0], [first] + kv_pieces[1:])

    total, attn_out = collect(partial, kv, attended)
    width = moe_x.shape[-1]
    return attn_out[None], total[None, :, :width], total[None, :, width:]


def solution(mesh):
    rows = P("seq", "group", "tp")
    tokens = P("group", ("seq", "tp"), None)
    experts = P(("seq", "tp"), None, None)
    return jax.shard_map(
        shards,
        mesh=mesh,
        in_specs=(rows, rows, rows, tokens, tokens, tokens, tokens, experts, experts, experts),
        out_specs=(rows, tokens, tokens),
        check_vma=False,
    )
```

```python
import functools
import math

import jax
import jax.numpy as jnp
from jax import lax
from jax.experimental import pallas as pl
from jax.experimental.pallas import tpu as pltpu
from jax.sharding import PartitionSpec as P

H = 32
KVH = 4
HD = 128
EXPERTS = 64
CAP = 3
NT = (((1,), (1,)), ((), ()))
VMEM = pl.BlockSpec(memory_space=pltpu.VMEM)
SMEM = pl.BlockSpec(memory_space=pltpu.SMEM)
ANY = pl.BlockSpec(memory_space=pl.ANY)
F32 = jnp.float32
BF16 = jnp.bfloat16


def swap(array, axis, offset):
    count = lax.axis_size(axis)
    return lax.ppermute(array, axis, [(i, i ^ offset) for i in range(count)])


def pack_kernel(ids_ref, gates_ref, x_ref, grad_ref, out_ref, own_ref):
    rows, width = x_ref.shape
    topk = ids_ref.shape[0]
    expert = lax.broadcasted_iota(jnp.int32, (EXPERTS, rows), 0)
    table = jnp.zeros((EXPERTS, rows), F32)
    for k in range(topk):
        table = table + jnp.where(ids_ref[k : k + 1] == expert, gates_ref[k : k + 1], 0.0)
    high = table.astype(BF16).astype(F32)
    both = jnp.concatenate([high, table - high], axis=0)
    both = jnp.transpose(both).astype(BF16)
    for ref in (out_ref, own_ref):
        ref[:, :width] = x_ref[...]
        ref[:, width : 2 * width] = grad_ref[...]
        ref[:, 2 * width :] = both


def pack_rows(ids, gates, x, grad):
    rows, width = x.shape
    return pl.pallas_call(
        pack_kernel,
        in_specs=[VMEM] * 4,
        out_specs=[VMEM] * 2,
        out_shape=[
            jax.ShapeDtypeStruct((rows, 2 * (width + EXPERTS)), BF16),
            pltpu.VMEM((rows, 2 * (width + EXPERTS)), BF16),
        ],
        name="pack_rows",
    )(ids, gates, x, grad)


def join_kernel(key_ref, value_ref, out_ref):
    half = key_ref.shape[1]
    out_ref[:, :half] = key_ref[...]
    out_ref[:, half:] = value_ref[...]


def join(keys, values):
    rows, half = keys.shape
    return pl.pallas_call(
        join_kernel,
        in_specs=[VMEM] * 2,
        out_specs=VMEM,
        out_shape=jax.ShapeDtypeStruct((rows, 2 * half), BF16),
        cost_estimate=pl.CostEstimate(flops=0, bytes_accessed=10**7, transcendentals=0),
        name="join",
    )(keys, values)


def attention_kernel(base_ref, q_ref, *refs):
    out_ref = refs[-1]
    kv_refs = refs[:-1]
    rows, width = q_ref.shape
    half = kv_refs[0].shape[1] // 2
    kv_heads = half // HD
    repeat = width // HD // kv_heads
    scale = math.log2(math.e) / HD**0.5
    row_pos = base_ref[0] * rows + lax.broadcasted_iota(jnp.int32, (rows, rows), 0)
    col_pos = lax.broadcasted_iota(jnp.int32, (rows, rows), 1)
    masks = [
        jnp.where(col_pos + base_ref[p] * rows <= row_pos, 0.0, -jnp.inf)
        for p in range(len(kv_refs))
    ]
    bias = jnp.concatenate(masks, axis=1)
    for g in range(kv_heads):
        keys = jnp.concatenate([r[:, g * HD : (g + 1) * HD] for r in kv_refs], axis=0)
        vals = jnp.concatenate(
            [r[:, half + g * HD : half + (g + 1) * HD] for r in kv_refs], axis=0
        )
        vals = jnp.concatenate([vals, jnp.ones_like(vals)], axis=1)
        for h in range(g * repeat, (g + 1) * repeat):
            cols = slice(h * HD, (h + 1) * HD)
            scores = lax.dot_general(q_ref[:, cols], keys, NT, preferred_element_type=F32) + bias
            top = jnp.max(scores, axis=1, keepdims=True)
            probs = jnp.exp2((scores - top) * scale).astype(BF16)
            mixed = jnp.dot(probs, vals, preferred_element_type=F32)
            out_ref[:, cols] = (mixed[:, :HD] / mixed[:, HD:]).astype(BF16)


def attend(base, q, kv):
    rows, width = q.shape
    keys = rows * len(kv)
    return pl.pallas_call(
        attention_kernel,
        in_specs=[SMEM] + [VMEM] * (1 + len(kv)),
        out_specs=VMEM,
        out_shape=jax.ShapeDtypeStruct((rows, width), BF16),
        cost_estimate=pl.CostEstimate(
            flops=4 * rows * keys * width, bytes_accessed=4 * rows * width, transcendentals=0
        ),
        name="attention",
    )(base, q, *kv)


def routing_rows(shard, gates, local, slots):
    tokens, lanes = gates.shape
    lane = lax.broadcasted_iota(jnp.int32, (local, lanes), 1)
    mine = shard * local + lax.broadcasted_iota(jnp.int32, (local, lanes), 0)
    columns = ((lane == mine) | (lane == mine + EXPERTS)).astype(BF16)
    weight = lax.dot_general(columns, gates, NT, preferred_element_type=F32)
    live = weight > 0
    earlier = lax.broadcasted_iota(jnp.int32, (tokens, tokens), 0)
    earlier = (earlier < lax.broadcasted_iota(jnp.int32, (tokens, tokens), 1)).astype(BF16)
    rank = jnp.dot(live.astype(BF16), earlier, preferred_element_type=F32)
    slot = lax.broadcasted_iota(jnp.int32, (slots, tokens), 0).astype(F32)
    picks, scales = [], []
    for e in range(local):
        pick = jnp.where((slot == rank[e : e + 1]) & live[e : e + 1], 1.0, 0.0)
        picks.append(pick)
        scales.append(jnp.sum(pick * weight[e : e + 1], axis=1, keepdims=True))
    return jnp.concatenate(picks, axis=0), jnp.concatenate(scales, axis=0)


def experts_kernel(shard_ref, *refs, count, slots):
    pieces = refs[:count]
    weights = refs[count : count + 3]
    outs = refs[count + 3 : 2 * count + 3]
    held, sems, tokens_scr, gates_scr, rows_scr, back_scr, scale_scr, pick_scr = refs[
        2 * count + 3 :
    ]
    gate_scr, up_scr, down_scr = held
    local, width, hidden = gate_scr.shape
    piece = pieces[0].shape[0]
    both = 2 * width

    def copy(which, e):
        return pltpu.make_async_copy(
            weights[which].at[e], held[which].at[e], sems.at[which, e]
        )

    for e in range(local):
        for which in range(3):
            copy(which, e).start()

    for p in range(count):
        tokens_scr[p * piece : (p + 1) * piece] = pieces[p][:, :both]
        gates_scr[p * piece : (p + 1) * piece] = pieces[p][:, both:]
    picks, scales = routing_rows(shard_ref[0], gates_scr[...], local, slots)
    scale_scr[...] = jnp.broadcast_to(scales, scale_scr.shape)
    high = scales.astype(BF16).astype(F32)
    for i, part in enumerate((picks, picks * high, picks * (scales - high))):
        pick_scr[i] = jnp.transpose(part).astype(BF16)
    picks = picks.astype(BF16)
    chunk = 512
    for c in range(0, both, chunk):
        rows_scr[:, c : c + chunk] = jnp.dot(
            picks, tokens_scr[:, c : c + chunk], preferred_element_type=F32
        ).astype(BF16)

    unroll = 2 if local % 2 == 0 else 1

    @pl.loop(0, local // unroll)
    def _(step):
        first = step * unroll
        for k in range(unroll):
            for which in range(3):
                copy(which, first + k).wait()
        every = pl.ds(pl.multiple_of(first * slots, slots), unroll * slots)
        down = down_scr.at[pl.ds(first, unroll)].reshape(unroll * hidden, width)
        row_grad = (rows_scr[every, width:].astype(F32) * scale_scr[every, :1]).astype(BF16)
        hidden_both, mine = [], []
        for k in range(unroll):
            mine.append(pl.ds(pl.multiple_of((first + k) * slots, slots), slots))
            entry = jnp.concatenate([gate_scr[first + k], up_scr[first + k]], axis=1)
            hidden_both.append(jnp.dot(rows_scr[mine[k], :width], entry, preferred_element_type=F32))
        grad_act = lax.dot_general(row_grad, down[...], NT, preferred_element_type=F32)
        activated = []
        for k in range(unroll):
            part = grad_act[k * slots : (k + 1) * slots, k * hidden : (k + 1) * hidden]
            hgate, hup = hidden_both[k][:, :hidden], hidden_both[k][:, hidden:]
            sig = jax.nn.sigmoid(hgate)
            silu = hgate * sig
            activated.append((silu * hup).astype(BF16))
            grad_gate = (part * hup * sig * (1.0 + hgate * (1.0 - sig))).astype(BF16)
            grad_up = (part * silu).astype(BF16)
            grads = jnp.concatenate([grad_gate, grad_up], axis=1)
            entry = jnp.concatenate([gate_scr[first + k], up_scr[first + k]], axis=1)
            back_scr[mine[k], width:] = lax.dot_general(
                grads, entry, NT, preferred_element_type=F32
            ).astype(BF16)
        blocks = [
            jnp.concatenate(
                [a if k == i else jnp.zeros_like(a) for i in range(unroll)], axis=1
            )
            for k, a in enumerate(activated)
        ]
        back_scr[every, :width] = jnp.dot(
            jnp.concatenate(blocks, axis=0), down[...], preferred_element_type=F32
        ).astype(BF16)

    for c in range(0, both, chunk):
        rows = back_scr[:, c : c + chunk]
        if c < width:
            total = jnp.dot(pick_scr[1], rows, preferred_element_type=F32)
            total = total + jnp.dot(pick_scr[2], rows, preferred_element_type=F32)
        else:
            total = jnp.dot(pick_scr[0], rows, preferred_element_type=F32)
        total = total.astype(BF16)
        for p in range(count):
            outs[p][:, c : c + chunk] = total[p * piece : (p + 1) * piece]


def experts(shard, pieces, w_gate, w_up, w_down):
    count = len(pieces)
    pieces = [pltpu.with_memory_space_constraint(pieces[0], pltpu.VMEM)] + pieces[1:]
    local, width, hidden = w_gate.shape
    piece = pieces[0].shape[0]
    tokens = count * piece
    slots = -(-CAP * count // 16) * 16
    scratch = [
        tuple(pltpu.VMEM(w.shape, BF16) for w in (w_gate, w_up, w_down)),
        pltpu.SemaphoreType.DMA((3, local)),
        pltpu.VMEM((tokens, 2 * width), BF16),
        pltpu.VMEM((tokens, pieces[0].shape[1] - 2 * width), BF16),
        pltpu.VMEM((local * slots, 2 * width), BF16),
        pltpu.VMEM((local * slots, 2 * width), BF16),
        pltpu.VMEM((local * slots, 128), F32),
        pltpu.VMEM((3, tokens, local * slots), BF16),
    ]
    held_bytes = 6 * local * width * hidden + 4 * width * (tokens + 2 * local * slots)
    return pl.pallas_call(
        functools.partial(experts_kernel, count=count, slots=slots),
        in_specs=[SMEM] + [VMEM] * count + [ANY] * 3,
        out_specs=[VMEM] * count,
        out_shape=[jax.ShapeDtypeStruct((piece, 2 * width), BF16)] * count,
        scratch_shapes=scratch,
        compiler_params=pltpu.CompilerParams(vmem_limit_bytes=held_bytes + 10 * 2**20),
        cost_estimate=pl.CostEstimate(
            flops=12 * local * slots * width * hidden,
            bytes_accessed=6 * local * width * hidden,
            transcendentals=0,
        ),
        name="experts",
    )(shard, *pieces, w_gate, w_up, w_down)


def parent(offset):
    return offset & (offset - 1)


def over_tp(block):
    return [swap(block, "tp", t) for t in range(1, lax.axis_size("tp"))]


def spread(rows, beside):
    near, far = [rows], []
    for d in range(1, lax.axis_size("seq")):
        block = swap(near[parent(d)], "seq", d - parent(d))
        if d == 1:
            rows, beside = lax.optimization_barrier((rows, beside))
            far.append(over_tp(rows))
        elif d == 2:
            far[0], near[1] = lax.optimization_barrier((far[0], near[1]))
            far.append([swap(a, "seq", 1) for a in far[0]])
        else:
            far.append(over_tp(near[d - 1]))
            block, far[: d - 2] = lax.optimization_barrier((block, far[: d - 2]))
        near.append(block)
    if len(near) == 2:
        far.append([swap(a, "seq", 1) for a in far[0]])
    elif len(near) > 2:
        far.append(over_tp(near[-1]))
    else:
        far.append(over_tp(rows))
    return near + [a for blocks in zip(*far) for a in blocks], beside


def collect(pieces, kv, beside):
    seq, tp = lax.axis_size("seq"), lax.axis_size("tp")
    terms = [[pieces[d]] for d in range(seq)]
    order = sorted(range(seq), key=lambda d: (-d.bit_count(), d))
    step = lax.axis_size("group") // 2
    kv, offsets = [kv], [0]
    last = None
    for d in order:
        terms[d] += [swap(pieces[t * seq + d], "tp", t) for t in range(1, tp)]
        if d == 0:
            break
        if last is not None:
            if step:
                kv = kv + [swap(a, "group", step) for a in kv]
                offsets = offsets + [o ^ step for o in offsets]
                step //= 2
            _, terms[d], kv = lax.optimization_barrier((last, terms[d], kv))
        last = sum(a.astype(F32) for a in terms[d]).astype(BF16)
        terms[parent(d)].append(swap(last, "seq", d - parent(d)))
    while step:
        kv = kv + [swap(a, "group", step) for a in kv]
        offsets = offsets + [o ^ step for o in offsets]
        step //= 2
    result = beside(last, kv, offsets)
    terms[0], result = lax.optimization_barrier((terms[0], result))
    return sum(a.astype(F32) for a in terms[0]).astype(BF16), result


def shards(queries, keys, values, moe_x, expert_ids, gates, grad_out, w_gate, w_up, w_down):
    group = lax.axis_index("group")
    shard = (lax.axis_index("seq") * lax.axis_size("tp") + lax.axis_index("tp")).reshape(1)
    rows, own = pack_rows(expert_ids[0].T, gates[0].T, moe_x[0], grad_out[0])
    pieces, kv = spread(rows, join(keys[0], values[0]))
    partial = experts(shard, [own] + pieces[1:], w_gate, w_up, w_down)
    partial, kv = lax.optimization_barrier((partial, kv))

    def attended(sums, kv_pieces, offsets):
        _, first = lax.optimization_barrier((sums, kv_pieces[0]))
        base = jnp.stack([group ^ d for d in offsets])
        return attend(base, queries[0], [first] + kv_pieces[1:])

    total, attn_out = collect(partial, kv, attended)
    width = moe_x.shape[-1]
    return attn_out[None], total[None, :, :width], total[None, :, width:]


def solution(mesh):
    rows = P("seq", "group", "tp")
    tokens = P("group", ("seq", "tp"), None)
    experts = P(("seq", "tp"), None, None)
    return jax.shard_map(
        shards,
        mesh=mesh,
        in_specs=(rows, rows, rows, tokens, tokens, tokens, tokens, experts, experts, experts),
        out_specs=(rows, tokens, tokens),
        check_vma=False,
    )
```

```python
import functools
import math

import jax
import jax.numpy as jnp
from jax import lax
from jax.experimental import pallas as pl
from jax.experimental.pallas import tpu as pltpu
from jax.sharding import PartitionSpec as P

H = 32
KVH = 4
HD = 128
EXPERTS = 64
CAP = 3
NT = (((1,), (1,)), ((), ()))
VMEM = pl.BlockSpec(memory_space=pltpu.VMEM)
SMEM = pl.BlockSpec(memory_space=pltpu.SMEM)
ANY = pl.BlockSpec(memory_space=pl.ANY)
F32 = jnp.float32
BF16 = jnp.bfloat16


def swap(array, axis, offset):
    count = lax.axis_size(axis)
    return lax.ppermute(array, axis, [(i, i ^ offset) for i in range(count)])


def pack_kernel(ids_ref, gates_ref, x_ref, grad_ref, out_ref, own_ref):
    rows, width = x_ref.shape
    topk = ids_ref.shape[0]
    expert = lax.broadcasted_iota(jnp.int32, (EXPERTS, rows), 0)
    table = jnp.zeros((EXPERTS, rows), F32)
    for k in range(topk):
        table = table + jnp.where(ids_ref[k : k + 1] == expert, gates_ref[k : k + 1], 0.0)
    high = table.astype(BF16).astype(F32)
    both = jnp.concatenate([high, table - high], axis=0)
    both = jnp.transpose(both).astype(BF16)
    for ref in (out_ref, own_ref):
        ref[:, :width] = x_ref[...]
        ref[:, width : 2 * width] = grad_ref[...]
        ref[:, 2 * width :] = both


def pack_rows(ids, gates, x, grad):
    rows, width = x.shape
    return pl.pallas_call(
        pack_kernel,
        in_specs=[VMEM] * 4,
        out_specs=[VMEM] * 2,
        out_shape=[
            pltpu.VMEM((rows, 2 * (width + EXPERTS)), BF16),
            pltpu.VMEM((rows, 2 * (width + EXPERTS)), BF16),
        ],
        name="pack_rows",
    )(ids, gates, x, grad)


def join_kernel(key_ref, value_ref, out_ref):
    half = key_ref.shape[1]
    out_ref[:, :half] = key_ref[...]
    out_ref[:, half:] = value_ref[...]


def join(keys, values):
    rows, half = keys.shape
    return pl.pallas_call(
        join_kernel,
        in_specs=[VMEM] * 2,
        out_specs=VMEM,
        out_shape=jax.ShapeDtypeStruct((rows, 2 * half), BF16),
        cost_estimate=pl.CostEstimate(flops=0, bytes_accessed=10**7, transcendentals=0),
        name="join",
    )(keys, values)


def attention_kernel(base_ref, q_ref, *refs):
    out_ref = refs[-1]
    kv_refs = refs[:-1]
    rows, width = q_ref.shape
    half = kv_refs[0].shape[1] // 2
    kv_heads = half // HD
    repeat = width // HD // kv_heads
    scale = math.log2(math.e) / HD**0.5
    row_pos = base_ref[0] * rows + lax.broadcasted_iota(jnp.int32, (rows, rows), 0)
    col_pos = lax.broadcasted_iota(jnp.int32, (rows, rows), 1)
    masks = [
        jnp.where(col_pos + base_ref[p] * rows <= row_pos, 0.0, -jnp.inf)
        for p in range(len(kv_refs))
    ]
    bias = jnp.concatenate(masks, axis=1)
    for g in range(kv_heads):
        keys = jnp.concatenate([r[:, g * HD : (g + 1) * HD] for r in kv_refs], axis=0)
        vals = jnp.concatenate(
            [r[:, half + g * HD : half + (g + 1) * HD] for r in kv_refs], axis=0
        )
        vals = jnp.concatenate([vals, jnp.ones_like(vals)], axis=1)
        for h in range(g * repeat, (g + 1) * repeat):
            cols = slice(h * HD, (h + 1) * HD)
            scores = lax.dot_general(q_ref[:, cols], keys, NT, preferred_element_type=F32) + bias
            top = jnp.max(scores, axis=1, keepdims=True)
            probs = jnp.exp2((scores - top) * scale).astype(BF16)
            mixed = jnp.dot(probs, vals, preferred_element_type=F32)
            out_ref[:, cols] = (mixed[:, :HD] / mixed[:, HD:]).astype(BF16)


def attend(base, q, kv):
    rows, width = q.shape
    keys = rows * len(kv)
    return pl.pallas_call(
        attention_kernel,
        in_specs=[SMEM] + [VMEM] * (1 + len(kv)),
        out_specs=VMEM,
        out_shape=jax.ShapeDtypeStruct((rows, width), BF16),
        cost_estimate=pl.CostEstimate(
            flops=4 * rows * keys * width, bytes_accessed=4 * rows * width, transcendentals=0
        ),
        name="attention",
    )(base, q, *kv)


def routing_rows(shard, gates, local, slots):
    tokens, lanes = gates.shape
    lane = lax.broadcasted_iota(jnp.int32, (local, lanes), 1)
    mine = shard * local + lax.broadcasted_iota(jnp.int32, (local, lanes), 0)
    columns = ((lane == mine) | (lane == mine + EXPERTS)).astype(BF16)
    weight = lax.dot_general(columns, gates, NT, preferred_element_type=F32)
    live = weight > 0
    earlier = lax.broadcasted_iota(jnp.int32, (tokens, tokens), 0)
    earlier = (earlier < lax.broadcasted_iota(jnp.int32, (tokens, tokens), 1)).astype(BF16)
    rank = jnp.dot(live.astype(BF16), earlier, preferred_element_type=F32)
    slot = lax.broadcasted_iota(jnp.int32, (slots, tokens), 0).astype(F32)
    picks, scales = [], []
    for e in range(local):
        pick = jnp.where((slot == rank[e : e + 1]) & live[e : e + 1], 1.0, 0.0)
        picks.append(pick)
        scales.append(jnp.sum(pick * weight[e : e + 1], axis=1, keepdims=True))
    return jnp.concatenate(picks, axis=0), jnp.concatenate(scales, axis=0)


def experts_kernel(shard_ref, *refs, count, slots):
    pieces = refs[:count]
    weights = refs[count : count + 3]
    outs = refs[count + 3 : 2 * count + 3]
    held, sems, rows_scr, back_scr, scale_scr, pick_scr = refs[
        2 * count + 3 :
    ]
    gate_scr, up_scr, down_scr = held
    local, width, hidden = gate_scr.shape
    piece = pieces[0].shape[0]
    both = 2 * width

    def copy(which, e):
        return pltpu.make_async_copy(
            weights[which].at[e], held[which].at[e], sems.at[which, e]
        )

    for e in range(local):
        for which in range(3):
            copy(which, e).start()

    gates = jnp.concatenate([r[:, both:] for r in pieces], axis=0)
    picks, scales = routing_rows(shard_ref[0], gates, local, slots)
    scale_scr[...] = jnp.broadcast_to(scales, scale_scr.shape)
    high = scales.astype(BF16).astype(F32)
    for i, part in enumerate((picks, picks * high, picks * (scales - high))):
        pick_scr[i] = jnp.transpose(part).astype(BF16)
    picks = picks.astype(BF16)
    chunk = 512
    for c in range(0, both, chunk):
        rows_scr[:, c : c + chunk] = jnp.dot(
            picks,
            jnp.concatenate([r[:, c : c + chunk] for r in pieces], axis=0),
            preferred_element_type=F32,
        ).astype(BF16)

    unroll = 2 if local % 2 == 0 else 1

    @pl.loop(0, local // unroll)
    def _(step):
        first = step * unroll
        for k in range(unroll):
            for which in range(3):
                copy(which, first + k).wait()
        every = pl.ds(pl.multiple_of(first * slots, slots), unroll * slots)
        down = down_scr.at[pl.ds(first, unroll)].reshape(unroll * hidden, width)
        row_grad = (rows_scr[every, width:].astype(F32) * scale_scr[every, :1]).astype(BF16)
        hidden_both, mine = [], []
        for k in range(unroll):
            mine.append(pl.ds(pl.multiple_of((first + k) * slots, slots), slots))
            entry = jnp.concatenate([gate_scr[first + k], up_scr[first + k]], axis=1)
            hidden_both.append(jnp.dot(rows_scr[mine[k], :width], entry, preferred_element_type=F32))
        grad_act = lax.dot_general(row_grad, down[...], NT, preferred_element_type=F32)
        activated = []
        for k in range(unroll):
            part = grad_act[k * slots : (k + 1) * slots, k * hidden : (k + 1) * hidden]
            hgate, hup = hidden_both[k][:, :hidden], hidden_both[k][:, hidden:]
            sig = jax.nn.sigmoid(hgate)
            silu = hgate * sig
            activated.append((silu * hup).astype(BF16))
            grad_gate = (part * hup * sig * (1.0 + hgate * (1.0 - sig))).astype(BF16)
            grad_up = (part * silu).astype(BF16)
            grads = jnp.concatenate([grad_gate, grad_up], axis=1)
            entry = jnp.concatenate([gate_scr[first + k], up_scr[first + k]], axis=1)
            back_scr[mine[k], width:] = lax.dot_general(
                grads, entry, NT, preferred_element_type=F32
            ).astype(BF16)
        blocks = [
            jnp.concatenate(
                [a if k == i else jnp.zeros_like(a) for i in range(unroll)], axis=1
            )
            for k, a in enumerate(activated)
        ]
        back_scr[every, :width] = jnp.dot(
            jnp.concatenate(blocks, axis=0), down[...], preferred_element_type=F32
        ).astype(BF16)

    for c in range(0, both, chunk):
        rows = back_scr[:, c : c + chunk]
        if c < width:
            total = jnp.dot(pick_scr[1], rows, preferred_element_type=F32)
            total = total + jnp.dot(pick_scr[2], rows, preferred_element_type=F32)
        else:
            total = jnp.dot(pick_scr[0], rows, preferred_element_type=F32)
        total = total.astype(BF16)
        for p in range(count):
            outs[p][:, c : c + chunk] = total[p * piece : (p + 1) * piece]


def experts(shard, pieces, w_gate, w_up, w_down):
    count = len(pieces)
    pieces = [pltpu.with_memory_space_constraint(pieces[0], pltpu.VMEM)] + pieces[1:]
    local, width, hidden = w_gate.shape
    piece = pieces[0].shape[0]
    tokens = count * piece
    slots = -(-CAP * count // 16) * 16
    scratch = [
        tuple(pltpu.VMEM(w.shape, BF16) for w in (w_gate, w_up, w_down)),
        pltpu.SemaphoreType.DMA((3, local)),
        pltpu.VMEM((local * slots, 2 * width), BF16),
        pltpu.VMEM((local * slots, 2 * width), BF16),
        pltpu.VMEM((local * slots, 128), F32),
        pltpu.VMEM((3, tokens, local * slots), BF16),
    ]
    held_bytes = 6 * local * width * hidden + 4 * width * (tokens + 2 * local * slots)
    return pl.pallas_call(
        functools.partial(experts_kernel, count=count, slots=slots),
        in_specs=[SMEM] + [VMEM] * count + [ANY] * 3,
        out_specs=[VMEM] * count,
        out_shape=[jax.ShapeDtypeStruct((piece, 2 * width), BF16)] * count,
        scratch_shapes=scratch,
        compiler_params=pltpu.CompilerParams(vmem_limit_bytes=held_bytes + 10 * 2**20),
        cost_estimate=pl.CostEstimate(
            flops=12 * local * slots * width * hidden,
            bytes_accessed=6 * local * width * hidden,
            transcendentals=0,
        ),
        name="experts",
    )(shard, *pieces, w_gate, w_up, w_down)


def parent(offset):
    return offset & (offset - 1)


def over_tp(block):
    return [swap(block, "tp", t) for t in range(1, lax.axis_size("tp"))]


def spread(rows, beside):
    near, far = [rows], []
    for d in range(1, lax.axis_size("seq")):
        block = swap(near[parent(d)], "seq", d - parent(d))
        if d == 1:
            rows, beside = lax.optimization_barrier((rows, beside))
            far.append(over_tp(rows))
        elif d == 2:
            far[0], near[1] = lax.optimization_barrier((far[0], near[1]))
            far.append([swap(a, "seq", 1) for a in far[0]])
        else:
            far.append(over_tp(near[d - 1]))
            block, far[: d - 2] = lax.optimization_barrier((block, far[: d - 2]))
        near.append(block)
    if len(near) == 2:
        far.append([swap(a, "seq", 1) for a in far[0]])
    elif len(near) > 2:
        far.append(over_tp(near[-1]))
    else:
        far.append(over_tp(rows))
    return near + [a for blocks in zip(*far) for a in blocks], beside


def collect(pieces, kv, beside):
    seq, tp = lax.axis_size("seq"), lax.axis_size("tp")
    terms = [[pieces[d]] for d in range(seq)]
    order = sorted(range(seq), key=lambda d: (-d.bit_count(), d))
    step = lax.axis_size("group") // 2
    kv, offsets = [kv], [0]
    last = None
    for d in order:
        terms[d] += [swap(pieces[t * seq + d], "tp", t) for t in range(1, tp)]
        if d == 0:
            break
        if last is not None:
            if step:
                kv = kv + [swap(a, "group", step) for a in kv]
                offsets = offsets + [o ^ step for o in offsets]
                step //= 2
            _, terms[d], kv = lax.optimization_barrier((last, terms[d], kv))
        last = sum(a.astype(F32) for a in terms[d]).astype(BF16)
        terms[parent(d)].append(swap(last, "seq", d - parent(d)))
    while step:
        kv = kv + [swap(a, "group", step) for a in kv]
        offsets = offsets + [o ^ step for o in offsets]
        step //= 2
    result = beside(last, kv, offsets)
    terms[0], result = lax.optimization_barrier((terms[0], result))
    return sum(a.astype(F32) for a in terms[0]).astype(BF16), result


def shards(queries, keys, values, moe_x, expert_ids, gates, grad_out, w_gate, w_up, w_down):
    group = lax.axis_index("group")
    shard = (lax.axis_index("seq") * lax.axis_size("tp") + lax.axis_index("tp")).reshape(1)
    rows, own = pack_rows(expert_ids[0].T, gates[0].T, moe_x[0], grad_out[0])
    pieces, kv = spread(rows, join(keys[0], values[0]))
    partial = experts(shard, [own] + pieces[1:], w_gate, w_up, w_down)
    partial, kv = lax.optimization_barrier((partial, kv))

    def attended(sums, kv_pieces, offsets):
        _, first = lax.optimization_barrier((sums, kv_pieces[0]))
        base = jnp.stack([group ^ d for d in offsets])
        return attend(base, queries[0], [first] + kv_pieces[1:])

    total, attn_out = collect(partial, kv, attended)
    width = moe_x.shape[-1]
    return attn_out[None], total[None, :, :width], total[None, :, width:]


def solution(mesh):
    rows = P("seq", "group", "tp")
    tokens = P("group", ("seq", "tp"), None)
    experts = P(("seq", "tp"), None, None)
    return jax.shard_map(
        shards,
        mesh=mesh,
        in_specs=(rows, rows, rows, tokens, tokens, tokens, tokens, experts, experts, experts),
        out_specs=(rows, tokens, tokens),
        check_vma=False,
    )
```

```python
import functools
import math

import jax
import jax.numpy as jnp
from jax import lax
from jax.experimental import pallas as pl
from jax.experimental.pallas import tpu as pltpu
from jax.sharding import PartitionSpec as P

H = 32
KVH = 4
HD = 128
EXPERTS = 64
CAP = 3
NT = (((1,), (1,)), ((), ()))
VMEM = pl.BlockSpec(memory_space=pltpu.VMEM)
SMEM = pl.BlockSpec(memory_space=pltpu.SMEM)
ANY = pl.BlockSpec(memory_space=pl.ANY)
F32 = jnp.float32
BF16 = jnp.bfloat16


def swap(array, axis, offset):
    count = lax.axis_size(axis)
    return lax.ppermute(array, axis, [(i, i ^ offset) for i in range(count)])


def pack_kernel(ids_ref, gates_ref, x_ref, grad_ref, out_ref, own_ref):
    rows, width = x_ref.shape
    topk = ids_ref.shape[0]
    expert = lax.broadcasted_iota(jnp.int32, (EXPERTS, rows), 0)
    table = jnp.zeros((EXPERTS, rows), F32)
    for k in range(topk):
        table = table + jnp.where(ids_ref[k : k + 1] == expert, gates_ref[k : k + 1], 0.0)
    high = table.astype(BF16).astype(F32)
    both = jnp.concatenate([high, table - high], axis=0)
    both = jnp.transpose(both).astype(BF16)
    for ref in (out_ref, own_ref):
        ref[:, :width] = x_ref[...]
        ref[:, width : 2 * width] = grad_ref[...]
        ref[:, 2 * width :] = both


def pack_rows(ids, gates, x, grad):
    rows, width = x.shape
    return pl.pallas_call(
        pack_kernel,
        in_specs=[VMEM] * 4,
        out_specs=[VMEM] * 2,
        out_shape=[
            pltpu.VMEM((rows, 2 * (width + EXPERTS)), BF16),
            pltpu.VMEM((rows, 2 * (width + EXPERTS)), BF16),
        ],
        name="pack_rows",
    )(ids, gates, x, grad)


def join_kernel(key_ref, value_ref, out_ref):
    half = key_ref.shape[1]
    out_ref[:, :half] = key_ref[...]
    out_ref[:, half:] = value_ref[...]


def join(keys, values):
    rows, half = keys.shape
    return pl.pallas_call(
        join_kernel,
        in_specs=[VMEM] * 2,
        out_specs=VMEM,
        out_shape=pltpu.VMEM((rows, 2 * half), BF16),
        cost_estimate=pl.CostEstimate(flops=0, bytes_accessed=8 * rows * half, transcendentals=0),
        name="join",
    )(keys, values)


def attention_kernel(base_ref, q_ref, *refs):
    out_ref = refs[-1]
    kv_refs = refs[:-1]
    rows, width = q_ref.shape
    half = kv_refs[0].shape[1] // 2
    kv_heads = half // HD
    repeat = width // HD // kv_heads
    scale = math.log2(math.e) / HD**0.5
    row_pos = base_ref[0] * rows + lax.broadcasted_iota(jnp.int32, (rows, rows), 0)
    col_pos = lax.broadcasted_iota(jnp.int32, (rows, rows), 1)
    masks = [
        jnp.where(col_pos + base_ref[p] * rows <= row_pos, 0.0, -jnp.inf)
        for p in range(len(kv_refs))
    ]
    bias = jnp.concatenate(masks, axis=1)
    for g in range(kv_heads):
        keys = jnp.concatenate([r[:, g * HD : (g + 1) * HD] for r in kv_refs], axis=0)
        vals = jnp.concatenate(
            [r[:, half + g * HD : half + (g + 1) * HD] for r in kv_refs], axis=0
        )
        vals = jnp.concatenate([vals, jnp.ones_like(vals)], axis=1)
        for h in range(g * repeat, (g + 1) * repeat):
            cols = slice(h * HD, (h + 1) * HD)
            scores = lax.dot_general(q_ref[:, cols], keys, NT, preferred_element_type=F32) + bias
            top = jnp.max(scores, axis=1, keepdims=True)
            probs = jnp.exp2((scores - top) * scale).astype(BF16)
            mixed = jnp.dot(probs, vals, preferred_element_type=F32)
            out_ref[:, cols] = (mixed[:, :HD] / mixed[:, HD:]).astype(BF16)


def attend(base, q, kv):
    rows, width = q.shape
    keys = rows * len(kv)
    return pl.pallas_call(
        attention_kernel,
        in_specs=[SMEM] + [VMEM] * (1 + len(kv)),
        out_specs=VMEM,
        out_shape=jax.ShapeDtypeStruct((rows, width), BF16),
        cost_estimate=pl.CostEstimate(
            flops=4 * rows * keys * width, bytes_accessed=4 * rows * width, transcendentals=0
        ),
        name="attention",
    )(base, q, *kv)


def routing_rows(shard, gates, local, slots):
    tokens, lanes = gates.shape
    lane = lax.broadcasted_iota(jnp.int32, (local, lanes), 1)
    mine = shard * local + lax.broadcasted_iota(jnp.int32, (local, lanes), 0)
    columns = ((lane == mine) | (lane == mine + EXPERTS)).astype(BF16)
    weight = lax.dot_general(columns, gates, NT, preferred_element_type=F32)
    live = weight > 0
    earlier = lax.broadcasted_iota(jnp.int32, (tokens, tokens), 0)
    earlier = (earlier < lax.broadcasted_iota(jnp.int32, (tokens, tokens), 1)).astype(BF16)
    rank = jnp.dot(live.astype(BF16), earlier, preferred_element_type=F32)
    slot = lax.broadcasted_iota(jnp.int32, (slots, tokens), 0).astype(F32)
    picks, scales = [], []
    for e in range(local):
        pick = jnp.where((slot == rank[e : e + 1]) & live[e : e + 1], 1.0, 0.0)
        picks.append(pick)
        scales.append(jnp.sum(pick * weight[e : e + 1], axis=1, keepdims=True))
    return jnp.concatenate(picks, axis=0), jnp.concatenate(scales, axis=0)


def experts_kernel(shard_ref, *refs, count, slots):
    pieces = refs[:count]
    weights = refs[count : count + 3]
    outs = refs[count + 3 : 2 * count + 3]
    held, sems, rows_scr, back_scr, scale_scr, pick_scr = refs[
        2 * count + 3 :
    ]
    gate_scr, up_scr, down_scr = held
    local, width, hidden = gate_scr.shape
    piece = pieces[0].shape[0]
    both = 2 * width

    def copy(which, e):
        return pltpu.make_async_copy(
            weights[which].at[e], held[which].at[e], sems.at[which, e]
        )

    for e in range(local):
        for which in range(3):
            copy(which, e).start()

    gates = jnp.concatenate([r[:, both:] for r in pieces], axis=0)
    picks, scales = routing_rows(shard_ref[0], gates, local, slots)
    scale_scr[...] = jnp.broadcast_to(scales, scale_scr.shape)
    high = scales.astype(BF16).astype(F32)
    for i, part in enumerate((picks, picks * high, picks * (scales - high))):
        pick_scr[i] = jnp.transpose(part).astype(BF16)
    picks = picks.astype(BF16)
    chunk = 512
    for c in range(0, both, chunk):
        rows_scr[:, c : c + chunk] = jnp.dot(
            picks,
            jnp.concatenate([r[:, c : c + chunk] for r in pieces], axis=0),
            preferred_element_type=F32,
        ).astype(BF16)

    unroll = 2 if local % 2 == 0 else 1

    @pl.loop(0, local // unroll)
    def _(step):
        first = step * unroll
        for k in range(unroll):
            for which in range(3):
                copy(which, first + k).wait()
        every = pl.ds(pl.multiple_of(first * slots, slots), unroll * slots)
        down = down_scr.at[pl.ds(first, unroll)].reshape(unroll * hidden, width)
        row_grad = (rows_scr[every, width:].astype(F32) * scale_scr[every, :1]).astype(BF16)
        hidden_both, mine = [], []
        for k in range(unroll):
            mine.append(pl.ds(pl.multiple_of((first + k) * slots, slots), slots))
            entry = jnp.concatenate([gate_scr[first + k], up_scr[first + k]], axis=1)
            hidden_both.append(jnp.dot(rows_scr[mine[k], :width], entry, preferred_element_type=F32))
        grad_act = lax.dot_general(row_grad, down[...], NT, preferred_element_type=F32)
        activated = []
        for k in range(unroll):
            part = grad_act[k * slots : (k + 1) * slots, k * hidden : (k + 1) * hidden]
            hgate, hup = hidden_both[k][:, :hidden], hidden_both[k][:, hidden:]
            sig = jax.nn.sigmoid(hgate)
            silu = hgate * sig
            activated.append((silu * hup).astype(BF16))
            grad_gate = (part * hup * sig * (1.0 + hgate * (1.0 - sig))).astype(BF16)
            grad_up = (part * silu).astype(BF16)
            grads = jnp.concatenate([grad_gate, grad_up], axis=1)
            entry = jnp.concatenate([gate_scr[first + k], up_scr[first + k]], axis=1)
            back_scr[mine[k], width:] = lax.dot_general(
                grads, entry, NT, preferred_element_type=F32
            ).astype(BF16)
        blocks = [
            jnp.concatenate(
                [a if k == i else jnp.zeros_like(a) for i in range(unroll)], axis=1
            )
            for k, a in enumerate(activated)
        ]
        back_scr[every, :width] = jnp.dot(
            jnp.concatenate(blocks, axis=0), down[...], preferred_element_type=F32
        ).astype(BF16)

    for c in range(0, both, chunk):
        rows = back_scr[:, c : c + chunk]
        if c < width:
            total = jnp.dot(pick_scr[1], rows, preferred_element_type=F32)
            total = total + jnp.dot(pick_scr[2], rows, preferred_element_type=F32)
        else:
            total = jnp.dot(pick_scr[0], rows, preferred_element_type=F32)
        total = total.astype(BF16)
        for p in range(count):
            outs[p][:, c : c + chunk] = total[p * piece : (p + 1) * piece]


def experts(shard, pieces, w_gate, w_up, w_down):
    count = len(pieces)
    pieces = [pltpu.with_memory_space_constraint(pieces[0], pltpu.VMEM)] + pieces[1:]
    local, width, hidden = w_gate.shape
    piece = pieces[0].shape[0]
    tokens = count * piece
    slots = -(-CAP * count // 16) * 16
    scratch = [
        tuple(pltpu.VMEM(w.shape, BF16) for w in (w_gate, w_up, w_down)),
        pltpu.SemaphoreType.DMA((3, local)),
        pltpu.VMEM((local * slots, 2 * width), BF16),
        pltpu.VMEM((local * slots, 2 * width), BF16),
        pltpu.VMEM((local * slots, 128), F32),
        pltpu.VMEM((3, tokens, local * slots), BF16),
    ]
    held_bytes = 6 * local * width * hidden + 4 * width * (tokens + 2 * local * slots)
    return pl.pallas_call(
        functools.partial(experts_kernel, count=count, slots=slots),
        in_specs=[SMEM] + [VMEM] * count + [ANY] * 3,
        out_specs=[VMEM] * count,
        out_shape=[jax.ShapeDtypeStruct((piece, 2 * width), BF16)] * count,
        scratch_shapes=scratch,
        compiler_params=pltpu.CompilerParams(vmem_limit_bytes=held_bytes + 10 * 2**20),
        cost_estimate=pl.CostEstimate(
            flops=12 * local * slots * width * hidden,
            bytes_accessed=6 * local * width * hidden,
            transcendentals=0,
        ),
        name="experts",
    )(shard, *pieces, w_gate, w_up, w_down)


def parent(offset):
    return offset & (offset - 1)


def over_tp(block):
    return [swap(block, "tp", t) for t in range(1, lax.axis_size("tp"))]


def spread(rows, beside):
    near, far = [rows], []
    later, beside = lax.optimization_barrier((rows, beside))
    for d in range(1, lax.axis_size("seq")):
        block = swap(near[parent(d)] if d > 1 else later, "seq", d - parent(d))
        if d == 1:
            far.append(over_tp(later))
        elif d == 2:
            far[0], near[1] = lax.optimization_barrier((far[0], near[1]))
            far.append([swap(a, "seq", 1) for a in far[0]])
        else:
            far.append(over_tp(near[d - 1]))
            block, far[: d - 2] = lax.optimization_barrier((block, far[: d - 2]))
        near.append(block)
    if len(near) == 1:
        far.append(over_tp(later))
    elif len(near) == 2:
        far.append([swap(a, "seq", 1) for a in far[0]])
    else:
        far.append(over_tp(near[-1]))
    return near + [a for blocks in zip(*far) for a in blocks], beside


def collect(pieces, kv, beside):
    seq, tp = lax.axis_size("seq"), lax.axis_size("tp")
    terms = [[pieces[d]] for d in range(seq)]
    order = sorted(range(seq), key=lambda d: (-d.bit_count(), d))
    step = lax.axis_size("group") // 2
    kv, offsets = [kv], [0]
    last = None
    for d in order:
        terms[d] += [swap(pieces[t * seq + d], "tp", t) for t in range(1, tp)]
        if d == 0:
            break
        if last is not None:
            if step:
                kv = kv + [swap(a, "group", step) for a in kv]
                offsets = offsets + [o ^ step for o in offsets]
                step //= 2
            _, terms[d], kv = lax.optimization_barrier((last, terms[d], kv))
        last = sum(a.astype(F32) for a in terms[d]).astype(BF16)
        terms[parent(d)].append(swap(last, "seq", d - parent(d)))
    while step:
        kv = kv + [swap(a, "group", step) for a in kv]
        offsets = offsets + [o ^ step for o in offsets]
        step //= 2
    result = beside(last, kv, offsets)
    terms[0], result = lax.optimization_barrier((terms[0], result))
    return sum(a.astype(F32) for a in terms[0]).astype(BF16), result


def shards(queries, keys, values, moe_x, expert_ids, gates, grad_out, w_gate, w_up, w_down):
    group = lax.axis_index("group")
    shard = (lax.axis_index("seq") * lax.axis_size("tp") + lax.axis_index("tp")).reshape(1)
    rows, own = pack_rows(expert_ids[0].T, gates[0].T, moe_x[0], grad_out[0])
    pieces, kv = spread(rows, join(keys[0], values[0]))
    partial = experts(shard, [own] + pieces[1:], w_gate, w_up, w_down)
    partial, kv = lax.optimization_barrier((partial, kv))

    def attended(sums, kv_pieces, offsets):
        _, first = lax.optimization_barrier((sums, kv_pieces[0]))
        base = jnp.stack([group ^ d for d in offsets])
        return attend(base, queries[0], [first] + kv_pieces[1:])

    total, attn_out = collect(partial, kv, attended)
    width = moe_x.shape[-1]
    return attn_out[None], total[None, :, :width], total[None, :, width:]


def solution(mesh):
    rows = P("seq", "group", "tp")
    tokens = P("group", ("seq", "tp"), None)
    experts = P(("seq", "tp"), None, None)
    return jax.shard_map(
        shards,
        mesh=mesh,
        in_specs=(rows, rows, rows, tokens, tokens, tokens, tokens, experts, experts, experts),
        out_specs=(rows, tokens, tokens),
        check_vma=False,
    )
```

```python
import functools
import math

import jax
import jax.numpy as jnp
from jax import lax
from jax.experimental import pallas as pl
from jax.experimental.pallas import tpu as pltpu
from jax.sharding import PartitionSpec as P

H = 32
KVH = 4
HD = 128
EXPERTS = 64
CAP = 3
NT = (((1,), (1,)), ((), ()))
VMEM = pl.BlockSpec(memory_space=pltpu.VMEM)
SMEM = pl.BlockSpec(memory_space=pltpu.SMEM)
ANY = pl.BlockSpec(memory_space=pl.ANY)
F32 = jnp.float32
BF16 = jnp.bfloat16


def swap(array, axis, offset):
    count = lax.axis_size(axis)
    return lax.ppermute(array, axis, [(i, i ^ offset) for i in range(count)])


def pack_kernel(ids_ref, gates_ref, x_ref, grad_ref, out_ref, own_ref):
    rows, width = x_ref.shape
    topk = ids_ref.shape[0]
    expert = lax.broadcasted_iota(jnp.int32, (EXPERTS, rows), 0)
    table = jnp.zeros((EXPERTS, rows), F32)
    for k in range(topk):
        table = table + jnp.where(ids_ref[k : k + 1] == expert, gates_ref[k : k + 1], 0.0)
    high = table.astype(BF16).astype(F32)
    both = jnp.concatenate([high, table - high], axis=0)
    both = jnp.transpose(both).astype(BF16)
    for ref in (out_ref, own_ref):
        ref[:, :width] = x_ref[...]
        ref[:, width : 2 * width] = grad_ref[...]
        ref[:, 2 * width :] = both


def pack_rows(ids, gates, x, grad):
    rows, width = x.shape
    return pl.pallas_call(
        pack_kernel,
        in_specs=[VMEM] * 4,
        out_specs=[VMEM] * 2,
        out_shape=[
            pltpu.VMEM((rows, 2 * (width + EXPERTS)), BF16),
            pltpu.VMEM((rows, 2 * (width + EXPERTS)), BF16),
        ],
        name="pack_rows",
    )(ids, gates, x, grad)


def join_kernel(key_ref, value_ref, out_ref):
    half = key_ref.shape[1]
    out_ref[:, :half] = key_ref[...]
    out_ref[:, half:] = value_ref[...]


def join(keys, values):
    rows, half = keys.shape
    return pl.pallas_call(
        join_kernel,
        in_specs=[VMEM] * 2,
        out_specs=VMEM,
        out_shape=pltpu.VMEM((rows, 2 * half), BF16),
        cost_estimate=pl.CostEstimate(flops=0, bytes_accessed=8 * rows * half, transcendentals=0),
        name="join",
    )(keys, values)


def attention_kernel(base_ref, q_ref, *refs):
    out_ref = refs[-1]
    kv_refs = refs[:-1]
    rows, width = q_ref.shape
    half = kv_refs[0].shape[1] // 2
    kv_heads = half // HD
    repeat = width // HD // kv_heads
    scale = math.log2(math.e) / HD**0.5
    row_pos = base_ref[0] * rows + lax.broadcasted_iota(jnp.int32, (rows, rows), 0)
    col_pos = lax.broadcasted_iota(jnp.int32, (rows, rows), 1)
    masks = [
        jnp.where(col_pos + base_ref[p] * rows <= row_pos, 0.0, -jnp.inf)
        for p in range(len(kv_refs))
    ]
    bias = jnp.concatenate(masks, axis=1)
    for g in range(kv_heads):
        keys = jnp.concatenate([r[:, g * HD : (g + 1) * HD] for r in kv_refs], axis=0)
        vals = jnp.concatenate(
            [r[:, half + g * HD : half + (g + 1) * HD] for r in kv_refs], axis=0
        )
        vals = jnp.concatenate([vals, jnp.ones_like(vals)], axis=1)
        for h in range(g * repeat, (g + 1) * repeat):
            cols = slice(h * HD, (h + 1) * HD)
            scores = lax.dot_general(q_ref[:, cols], keys, NT, preferred_element_type=F32) + bias
            top = jnp.max(scores, axis=1, keepdims=True)
            probs = jnp.exp2((scores - top) * scale).astype(BF16)
            mixed = jnp.dot(probs, vals, preferred_element_type=F32)
            out_ref[:, cols] = (mixed[:, :HD] / mixed[:, HD:]).astype(BF16)


def attend(base, q, kv):
    rows, width = q.shape
    keys = rows * len(kv)
    return pl.pallas_call(
        attention_kernel,
        in_specs=[SMEM] + [VMEM] * (1 + len(kv)),
        out_specs=VMEM,
        out_shape=jax.ShapeDtypeStruct((rows, width), BF16),
        cost_estimate=pl.CostEstimate(
            flops=4 * rows * keys * width, bytes_accessed=4 * rows * width, transcendentals=0
        ),
        name="attention",
    )(base, q, *kv)


def routing_rows(shard, gates, local, slots):
    tokens, lanes = gates.shape
    lane = lax.broadcasted_iota(jnp.int32, (local, lanes), 1)
    mine = shard * local + lax.broadcasted_iota(jnp.int32, (local, lanes), 0)
    columns = ((lane == mine) | (lane == mine + EXPERTS)).astype(BF16)
    weight = lax.dot_general(columns, gates, NT, preferred_element_type=F32)
    live = weight > 0
    earlier = lax.broadcasted_iota(jnp.int32, (tokens, tokens), 0)
    earlier = (earlier < lax.broadcasted_iota(jnp.int32, (tokens, tokens), 1)).astype(BF16)
    rank = jnp.dot(live.astype(BF16), earlier, preferred_element_type=F32)
    slot = lax.broadcasted_iota(jnp.int32, (slots, tokens), 0).astype(F32)
    picks, scales = [], []
    for e in range(local):
        pick = jnp.where((slot == rank[e : e + 1]) & live[e : e + 1], 1.0, 0.0)
        picks.append(pick)
        scales.append(jnp.sum(pick * weight[e : e + 1], axis=1, keepdims=True))
    return jnp.concatenate(picks, axis=0), jnp.concatenate(scales, axis=0)


def experts_kernel(shard_ref, *refs, count, slots):
    pieces = refs[:count]
    weights = refs[count : count + 3]
    outs = refs[count + 3 : 2 * count + 3]
    held, sems, rows_scr, back_scr, scale_scr, pick_scr = refs[
        2 * count + 3 :
    ]
    gate_scr, up_scr, down_scr = held
    local, width, hidden = gate_scr.shape
    piece = pieces[0].shape[0]
    both = 2 * width

    def copy(which, e):
        return pltpu.make_async_copy(
            weights[which].at[e], held[which].at[e], sems.at[which, e]
        )

    for e in range(local):
        for which in range(3):
            copy(which, e).start()

    gates = jnp.concatenate([r[:, both:] for r in pieces], axis=0)
    picks, scales = routing_rows(shard_ref[0], gates, local, slots)
    scale_scr[...] = jnp.broadcast_to(scales, scale_scr.shape)
    high = scales.astype(BF16).astype(F32)
    for i, part in enumerate((picks, picks * high, picks * (scales - high))):
        pick_scr[i] = jnp.transpose(part).astype(BF16)
    picks = picks.astype(BF16)
    chunk = 512
    for c in range(0, both, chunk):
        rows_scr[:, c : c + chunk] = jnp.dot(
            picks,
            jnp.concatenate([r[:, c : c + chunk] for r in pieces], axis=0),
            preferred_element_type=F32,
        ).astype(BF16)

    unroll = 2 if local % 2 == 0 else 1

    @pl.loop(0, local // unroll)
    def _(step):
        first = step * unroll
        for k in range(unroll):
            for which in range(3):
                copy(which, first + k).wait()
        every = pl.ds(pl.multiple_of(first * slots, slots), unroll * slots)
        down = down_scr.at[pl.ds(first, unroll)].reshape(unroll * hidden, width)
        row_grad = (rows_scr[every, width:].astype(F32) * scale_scr[every, :1]).astype(BF16)
        hidden_both, mine = [], []
        for k in range(unroll):
            mine.append(pl.ds(pl.multiple_of((first + k) * slots, slots), slots))
            entry = jnp.concatenate([gate_scr[first + k], up_scr[first + k]], axis=1)
            hidden_both.append(jnp.dot(rows_scr[mine[k], :width], entry, preferred_element_type=F32))
        grad_act = lax.dot_general(row_grad, down[...], NT, preferred_element_type=F32)
        activated = []
        for k in range(unroll):
            part = grad_act[k * slots : (k + 1) * slots, k * hidden : (k + 1) * hidden]
            hgate, hup = hidden_both[k][:, :hidden], hidden_both[k][:, hidden:]
            sig = jax.nn.sigmoid(hgate)
            silu = hgate * sig
            activated.append((silu * hup).astype(BF16))
            grad_gate = (part * hup * sig * (1.0 + hgate * (1.0 - sig))).astype(BF16)
            grad_up = (part * silu).astype(BF16)
            grads = jnp.concatenate([grad_gate, grad_up], axis=1)
            entry = jnp.concatenate([gate_scr[first + k], up_scr[first + k]], axis=1)
            back_scr[mine[k], width:] = lax.dot_general(
                grads, entry, NT, preferred_element_type=F32
            ).astype(BF16)
        blocks = [
            jnp.concatenate(
                [a if k == i else jnp.zeros_like(a) for i in range(unroll)], axis=1
            )
            for k, a in enumerate(activated)
        ]
        back_scr[every, :width] = jnp.dot(
            jnp.concatenate(blocks, axis=0), down[...], preferred_element_type=F32
        ).astype(BF16)

    for c in range(0, both, chunk):
        rows = back_scr[:, c : c + chunk]
        if c < width:
            total = jnp.dot(pick_scr[1], rows, preferred_element_type=F32)
            total = total + jnp.dot(pick_scr[2], rows, preferred_element_type=F32)
        else:
            total = jnp.dot(pick_scr[0], rows, preferred_element_type=F32)
        total = total.astype(BF16)
        for p in range(count):
            outs[p][:, c : c + chunk] = total[p * piece : (p + 1) * piece]


def experts(shard, pieces, w_gate, w_up, w_down):
    count = len(pieces)
    pieces = [pltpu.with_memory_space_constraint(pieces[0], pltpu.VMEM)] + pieces[1:]
    local, width, hidden = w_gate.shape
    piece = pieces[0].shape[0]
    tokens = count * piece
    slots = -(-CAP * count // 16) * 16
    scratch = [
        tuple(pltpu.VMEM(w.shape, BF16) for w in (w_gate, w_up, w_down)),
        pltpu.SemaphoreType.DMA((3, local)),
        pltpu.VMEM((local * slots, 2 * width), BF16),
        pltpu.VMEM((local * slots, 2 * width), BF16),
        pltpu.VMEM((local * slots, 128), F32),
        pltpu.VMEM((3, tokens, local * slots), BF16),
    ]
    held_bytes = 6 * local * width * hidden + 4 * width * (tokens + 2 * local * slots)
    return pl.pallas_call(
        functools.partial(experts_kernel, count=count, slots=slots),
        in_specs=[SMEM] + [VMEM] * count + [ANY] * 3,
        out_specs=[VMEM] * count,
        out_shape=[jax.ShapeDtypeStruct((piece, 2 * width), BF16)] * count,
        scratch_shapes=scratch,
        compiler_params=pltpu.CompilerParams(vmem_limit_bytes=held_bytes + 10 * 2**20),
        cost_estimate=pl.CostEstimate(
            flops=12 * local * slots * width * hidden,
            bytes_accessed=6 * local * width * hidden,
            transcendentals=0,
        ),
        name="experts",
    )(shard, *pieces, w_gate, w_up, w_down)


def parent(offset):
    return offset & (offset - 1)


def over_tp(block):
    return [swap(block, "tp", t) for t in range(1, lax.axis_size("tp"))]


def spread(rows, beside):
    near, far = [rows], []
    later, beside = lax.optimization_barrier((rows, beside))
    for d in range(1, lax.axis_size("seq")):
        block = swap(near[parent(d)] if d > 1 else later, "seq", d - parent(d))
        if d == 1:
            far.append(over_tp(later))
        elif d == 2:
            far[0], near[1] = lax.optimization_barrier((far[0], near[1]))
            far.append([swap(a, "seq", 1) for a in far[0]])
        else:
            far.append(over_tp(near[d - 1]))
            block, far[: d - 2] = lax.optimization_barrier((block, far[: d - 2]))
        near.append(block)
    if len(near) == 1:
        far.append(over_tp(later))
    elif len(near) == 2:
        far.append([swap(a, "seq", 1) for a in far[0]])
    else:
        far.append(over_tp(near[-1]))
    return near + [a for blocks in zip(*far) for a in blocks], beside


def collect(pieces, kv, beside):
    seq, tp = lax.axis_size("seq"), lax.axis_size("tp")
    terms = [[pieces[d]] for d in range(seq)]
    order = sorted(range(seq), key=lambda d: (-d.bit_count(), -d))
    step = lax.axis_size("group") // 2
    kv, offsets = [kv], [0]
    last = None
    for d in order:
        terms[d] += [swap(pieces[t * seq + d], "tp", t) for t in range(1, tp)]
        if d == 0:
            break
        if last is not None:
            if step:
                kv = kv + [swap(a, "group", step) for a in kv]
                offsets = offsets + [o ^ step for o in offsets]
                step //= 2
            _, terms[d], kv = lax.optimization_barrier((last, terms[d], kv))
        last = sum(a.astype(F32) for a in terms[d]).astype(BF16)
        terms[parent(d)].append(swap(last, "seq", d - parent(d)))
    while step:
        kv = kv + [swap(a, "group", step) for a in kv]
        offsets = offsets + [o ^ step for o in offsets]
        step //= 2
    result = beside(last, kv, offsets)
    terms[0], result = lax.optimization_barrier((terms[0], result))
    return sum(a.astype(F32) for a in terms[0]).astype(BF16), result


def shards(queries, keys, values, moe_x, expert_ids, gates, grad_out, w_gate, w_up, w_down):
    group = lax.axis_index("group")
    shard = (lax.axis_index("seq") * lax.axis_size("tp") + lax.axis_index("tp")).reshape(1)
    rows, own = pack_rows(expert_ids[0].T, gates[0].T, moe_x[0], grad_out[0])
    pieces, kv = spread(rows, join(keys[0], values[0]))
    partial = experts(shard, [own] + pieces[1:], w_gate, w_up, w_down)
    partial, kv = lax.optimization_barrier((partial, kv))

    def attended(sums, kv_pieces, offsets):
        _, first = lax.optimization_barrier((sums, kv_pieces[0]))
        base = jnp.stack([group ^ d for d in offsets])
        return attend(base, queries[0], [first] + kv_pieces[1:])

    total, attn_out = collect(partial, kv, attended)
    width = moe_x.shape[-1]
    return attn_out[None], total[None, :, :width], total[None, :, width:]


def solution(mesh):
    rows = P("seq", "group", "tp")
    tokens = P("group", ("seq", "tp"), None)
    experts = P(("seq", "tp"), None, None)
    return jax.shard_map(
        shards,
        mesh=mesh,
        in_specs=(rows, rows, rows, tokens, tokens, tokens, tokens, experts, experts, experts),
        out_specs=(rows, tokens, tokens),
        check_vma=False,
    )
```
